32 devices in a mesh: req: 4 (over z), ep: 8 (over y, x, core).
Axes of the slice: x: 2, y: 2, z: 4, core: 2. Of those that a mesh axis runs over, the one named last changes fastest.
Arguments:
- queries: bfloat16 [1024, 16, 192], P('ep'), may hold values from -260 to 260
- draft_latent: bfloat16 [1024, 576], P('ep'), may hold values from -5 to 5
- hidden_in: bfloat16 [1024, 2048], P('ep', 'req'), may hold values from -36 to 36
- cache_pool: bfloat16 [512, 128, 576], P(('req', 'ep')), may hold values from -5 to 5
- page_table: int32 [16, 32], P('ep'), may hold values from 0 to 15, as said below
- cache_len: int32 [16], P('ep'), may hold values from 1 to 3584
- parents: int32 [16, 64], P('ep'), may hold values from -1 to 62, as said below
- accept_leaf: int32 [16], P('ep'), may hold values from 0 to 63
- absorb_key: bfloat16 [16, 128, 512], replicated, may hold values from -0.5 to 0.5
- absorb_value: bfloat16 [16, 512, 128], replicated, may hold values from -0.25 to 0.25
- out_proj: bfloat16 [2048, 2048], P(None, 'req'), may hold values from -0.125 to 0.125
- norm_gain: float32 [2048], replicated, may hold values from 0.1 to 1.9
- router: bfloat16 [2048, 16], replicated, may hold values from -0.125 to 0.125
- expert_ids: int32 [1024, 6], P('ep'), may hold values from 0 to 15, all different within a row; in each aligned block of 128 rows (0 to 127, 128 to 255, ...) at most 96 rows name the same one
- expert_gate_up: bfloat16 [16, 2, 2048, 1408], P('ep', None, None, 'req'), may hold values from -0.125 to 0.125
- expert_down: bfloat16 [16, 1408, 2048], P('ep', 'req'), may hold values from -0.15625 to 0.15625
- shared_gate_up: bfloat16 [2, 2048, 1408], P(None, None, 'req'), may hold values from -0.125 to 0.125
- shared_down: bfloat16 [1408, 2048], P('req'), may hold values from -0.15625 to 0.15625
Outputs:
- layer_out: bfloat16 [1024, 2048], P('ep', 'req')
- new_pages: bfloat16 [16, 4, 128, 576], P('ep', 'req')
The draws below stay inside these ranges and needn't reach their ends.
Inputs may be any that keep to these rules, and one draw needn't show every extreme that they name: `page_table`: for the 2 requests of one ep index, the pages j with one value of j mod 4 name distinct slots. parents[r, i] < i, and it is -1 exactly at i = 0. `expert_ids`: in each aligned block of 128 rows no expert is named by more than 96 rows.
All inputs are finite; a program needn't handle non-finite values.
Results may differ from the reference program's by a relative error of at most 0.011.
Values may be sent and summed in bfloat16 or wider, within the bound.
A program may use at most 128 MiB of HBM per device.

```python
import math
import jax
import jax.numpy as jnp
import numpy as np
from jax import lax

D = 2048
H = 16
QK_NOPE = 128
ROPE = 64
V_HEAD = 128
LAT = 512
FF = 1408
TOPK = 6
SFF = 1408
PAGE = 128
DRAFT = 64
REQ_DEV = 2
MAX_LEN = 4096
KV = 576
EXPERTS = 16
TOK_EP = 128
REQUESTS = 16
TOKENS = 1024
MAXP = 32
POOL_DEV = 16
POOL = 512
LMAX = 3584
CAP = 96
N_REQ = 4
N_EP = 8


def draw_queries(key, part):
    first = jax.random.fold_in(jax.random.fold_in(key, 1), 0)
    return jnp.clip(jax.random.normal(first, (TOKENS, H, QK_NOPE + ROPE), jnp.float32), -6.0, 6.0).astype(jnp.bfloat16)


def draw_cache_pool(key, part):
    first = jax.random.fold_in(jax.random.fold_in(key, 2), 0)
    return jnp.clip(jax.random.normal(first, (POOL, PAGE, LAT + ROPE), jnp.float32), -5.0, 5.0).astype(jnp.bfloat16)


def draw_hidden_in(key, part):
    first, second, third = jax.random.split(jax.random.fold_in(key, 3), 3)
    row_scale = jnp.exp(jax.random.uniform(first, (TOKENS, 1), jnp.float32, math.log(0.3), math.log(3.0)))
    col_scale = jnp.exp(jax.random.uniform(second, (1, D), jnp.float32, math.log(0.3), math.log(3.0)))
    base = jnp.clip(jax.random.normal(third, (TOKENS, D), jnp.float32), -4.0, 4.0)
    return (base * row_scale * col_scale).astype(jnp.bfloat16)


def draw_page_table(key, part):
    streams = jax.random.split(jax.random.fold_in(key, 7), N_EP * N_REQ)
    shuffled = jax.vmap(lambda stream: jax.random.permutation(stream, POOL_DEV))(streams)
    shuffled = shuffled.reshape(N_EP, N_REQ, REQ_DEV, MAXP // N_REQ)
    table = jnp.transpose(shuffled, (0, 2, 3, 1)).reshape(REQUESTS, MAXP)
    return table.astype(jnp.int32)


def draw_cache_len(key, part):
    first, second, third = jax.random.split(jax.random.fold_in(key, 9), 3)
    longer = jax.random.randint(first, (REQUESTS,), 1, LMAX + 1)
    shorter = jax.random.randint(second, (REQUESTS,), 1, LMAX // 8 + 1)
    picked = jax.random.randint(third, (REQUESTS,), 0, 2)
    lengths = jnp.where(picked == 1, longer, shorter)
    return lengths.at[0].set(LMAX).astype(jnp.int32)


def draw_parents(key, part):
    draft_index = jnp.arange(DRAFT, dtype=jnp.int32)
    upper = jnp.maximum(jnp.minimum(draft_index, 4), 1) + 1
    backward = jax.random.randint(jax.random.fold_in(key, 11), (REQUESTS, DRAFT), 1, upper[None, :])
    return (draft_index[None, :] - backward).astype(jnp.int32)


def place_ends(values, stream_key, low, largest):
    longest = values.shape.index(max(values.shape))
    spots = []
    for shift in (0, 1):
        where = [jax.random.randint(jax.random.fold_in(stream_key, axis), (), 0, length) for axis, length in enumerate(values.shape)]
        where[longest] = (where[longest] + shift) % values.shape[longest]
        spots.append(tuple(where))
    return values.at[spots[0]].set(low).at[spots[1]].set(largest)


def levels(stream_key, shape, cuts, least, largest):
    def one(axis_at, shards_of):
        draws = jax.random.uniform(jax.random.fold_in(jax.random.fold_in(stream_key, 6), axis_at), (shards_of,), jnp.float32, least / len(cuts), largest / len(cuts))
        return jnp.repeat(jnp.exp(draws), shape[axis_at] // shards_of).reshape((-1,) + (1,) * (len(shape) - axis_at - 1))

    gain = one(*cuts[0])
    for cut in cuts[1:]:
        gain = gain * one(*cut)
    return gain


def deal_out(key, own, number, rows, count, top, limit, lean):
    order = jax.random.permutation(key, count)
    heavy_load, usual = shares(count, rows * top, limit, lean, True), shares(count, rows * top, limit, lean, False)
    places = jnp.arange(count)

    def named(sizes, rotation):
        used = int((sizes > 0).sum())
        fixed = max(1, used // 4)
        passed = fixed + (places - fixed + rotation * (used - fixed)) % max(1, count - fixed)
        return jnp.zeros((count,), jnp.int32).at[order[jnp.where(places < fixed, places, passed)]].set(jnp.asarray(sizes, jnp.int32))

    sizes = jnp.where(number % 4 == 0, named(heavy_load, number // 4), named(usual, number - number // 4 - 1))
    mixed = jax.random.permutation(jax.random.fold_in(own, 3), count)
    giver, taker = mixed[0:count // 2 * 2:2], mixed[1:count // 2 * 2:2]
    slack = jnp.minimum(sizes[giver] - 1, limit - sizes[taker]) // 2
    slack = jnp.where((giver == order[0]) | (taker == order[0]) | (sizes[taker] == 0), 0, jnp.maximum(slack, 0))
    passed = jax.random.randint(jax.random.fold_in(own, 4), (count // 2,), 0, 1 << 20) % (slack + 1)
    sizes = sizes.at[giver].add(-passed).at[taker].add(passed)
    members = jnp.searchsorted(jnp.cumsum(sizes), jnp.arange(rows * top), side="right").astype(jnp.int32)
    listing = members.reshape(top, rows).T
    listing = listing[jax.random.permutation(jax.random.fold_in(own, 1), rows)]
    rotation = jax.random.randint(jax.random.fold_in(own, 2), (rows, 1), 0, top)
    return jnp.take_along_axis(listing, (jnp.arange(top)[None, :] + rotation) % top, axis=1)


def shares(count, total, bound, skew, full):
    portions = [(1 << 20) // math.isqrt(grade ** skew) + 1 for grade in range(1, count + 1)]
    largest = bound if full else min(bound, max(-(-total // count), total * portions[0] // sum(portions)))
    least = 1 if total - largest >= count - 1 else 0
    counts, spare = [largest] + [least] * (count - 1), total - largest - least * (count - 1)
    while spare > 0:
        free = [i for i in range(1, count) if counts[i] < largest] or [i for i in range(1, count) if counts[i] < bound]
        pool, budget = sum([portions[i] for i in free]), spare
        for i in free:
            extra = min(bound - counts[i], max(1, budget * portions[i] // pool), spare)
            counts[i] = counts[i] + extra
            spare = spare - extra
    return np.array(counts)


def normal_values(rng, extent, scale, bound, cuts=(), kind=jnp.bfloat16):
    gain = levels(rng, extent, cuts, -0.22, 0.18) if cuts else 1.0
    values = jax.random.normal(rng, extent, jnp.float32) * scale * gain
    return jnp.minimum(jnp.maximum(values, -bound), bound).astype(kind)


def setup_inputs(seed: int = 0) -> dict:
    key_list = jax.random.split(jax.random.key(seed), 19)
    queries = draw_queries(jax.random.fold_in(key_list[18], 71), 0)
    draft_latent = normal_values(key_list[1], (TOKENS, KV), 1.0, 5.0, ((0, 8),))
    hidden_in = draw_hidden_in(jax.random.fold_in(key_list[18], 71), 0)
    cache_pool = draw_cache_pool(jax.random.fold_in(key_list[18], 71), 0)
    page_table = draw_page_table(jax.random.fold_in(key_list[18], 71), 0)
    cache_len = draw_cache_len(jax.random.fold_in(key_list[18], 71), 0)
    parents = draw_parents(jax.random.fold_in(key_list[18], 71), 0)
    accept_leaf = place_ends(jax.random.randint(key_list[7], (REQUESTS,), 0, DRAFT), jax.random.fold_in(key_list[7], 1), 0, DRAFT - 1).astype(jnp.int32)
    absorb_key = normal_values(key_list[8], (H, QK_NOPE, LAT), QK_NOPE ** -0.5, 0.5)
    absorb_value = normal_values(key_list[9], (H, LAT, V_HEAD), LAT ** -0.5, 0.25)
    out_proj = normal_values(key_list[10], (H * V_HEAD, D), (H * V_HEAD) ** -0.5, 0.125, ((1, 4),))
    norm_gain = jnp.clip(1.0 + 0.18 * jax.random.normal(key_list[11], (D,), jnp.float32), 0.1, 1.9)
    router = normal_values(key_list[12], (D, EXPERTS), D ** -0.5, 0.125)
    expert_ids_keys = jax.random.split(jax.random.fold_in(key_list[13], 1), TOKENS // TOK_EP)
    expert_ids_turns = jax.random.permutation(jax.random.fold_in(key_list[13], 3), TOKENS // TOK_EP)
    expert_ids = jax.vmap(lambda own, number: deal_out(jax.random.fold_in(key_list[13], 2), own, number, TOK_EP, EXPERTS, TOPK, CAP, 2))(expert_ids_keys, expert_ids_turns).reshape((TOKENS, TOPK))
    expert_gate_up = normal_values(key_list[14], (EXPERTS, 2, D, FF), D ** -0.5, 0.125, ((0, 8), (3, 4)))
    expert_down = normal_values(key_list[15], (EXPERTS, FF, D), FF ** -0.5, 0.15625, ((0, 8), (1, 4)))
    shared_gate_up = normal_values(key_list[16], (2, D, SFF), D ** -0.5, 0.125, ((2, 4),))
    shared_down = normal_values(key_list[17], (SFF, D), SFF ** -0.5, 0.15625, ((0, 4),))
    return dict(queries=queries, draft_latent=draft_latent, hidden_in=hidden_in, cache_pool=cache_pool, page_table=page_table, cache_len=cache_len, parents=parents, accept_leaf=accept_leaf, absorb_key=absorb_key, absorb_value=absorb_value, out_proj=out_proj, norm_gain=norm_gain, router=router, expert_ids=expert_ids, expert_gate_up=expert_gate_up, expert_down=expert_down, shared_gate_up=shared_gate_up, shared_down=shared_down)


def ancestors(parents):
    draft_count = parents.shape[-1]
    draft_index = jnp.arange(draft_count, dtype=jnp.int32)
    ancestry = (parents[:, :, None] == draft_index[None, None, :]).astype(jnp.float32)
    ancestry = ancestry + jnp.eye(draft_count, dtype=jnp.float32)[None]
    for doubling in range(max(1, (draft_count - 1).bit_length())):
        ancestry = jnp.minimum(jnp.einsum('rij,rjk->rik', ancestry, ancestry, precision=lax.Precision.HIGHEST), 1.0)
    return ancestry

def reference(queries, draft_latent, hidden_in, cache_pool, page_table, cache_len, parents, accept_leaf, absorb_key, absorb_value, out_proj, norm_gain, router, expert_ids, expert_gate_up, expert_down, shared_gate_up, shared_down):
    highest = lax.Precision.HIGHEST
    ancestry = ancestors(parents)
    depths = lax.optimization_barrier(jnp.sum(ancestry, axis=2)) - 1.0
    score_scale = 1.0 / math.sqrt(QK_NOPE + ROPE)
    page_index = jnp.arange(MAXP, dtype=jnp.int32)
    groups = jnp.arange(REQUESTS, dtype=jnp.int32) // REQ_DEV
    owners = page_index[None, :] % N_REQ * N_EP + groups[:, None]
    global_pages = (owners * POOL_DEV + page_table).astype(jnp.int32)
    positions = jnp.arange(MAX_LEN, dtype=jnp.int32)
    key_weight = absorb_key.astype(jnp.float32)
    value_weight = absorb_value.astype(jnp.float32)

    def one_request(request_items):
        page_rows, length, tree_mask, query_rows, drafts = request_items
        cached = cache_pool[page_rows].reshape(MAX_LEN, KV).astype(jnp.float32)
        absorbed = jnp.einsum('thd,hdl->thl', query_rows[:, :, :QK_NOPE].astype(jnp.float32), key_weight)
        absorbed = lax.optimization_barrier(absorbed.astype(jnp.bfloat16))
        query_full = jnp.concatenate([absorbed, query_rows[:, :, QK_NOPE:]], axis=2).astype(jnp.float32)
        draft_keys = drafts.astype(jnp.float32)
        cache_ok = positions < length
        tree_ok = tree_mask > 0.5
        score_cache = jnp.einsum('thk,sk->ths', query_full, cached) * score_scale
        score_cache = jnp.where(cache_ok[None, None, :], score_cache, -jnp.inf)
        score_draft = jnp.einsum('thk,sk->ths', query_full, draft_keys) * score_scale
        score_draft = jnp.where(tree_ok[:, None, :], score_draft, -jnp.inf)
        highest_score = jnp.maximum(lax.optimization_barrier(jnp.max(score_cache, axis=2)), lax.optimization_barrier(jnp.max(score_draft, axis=2)))
        weight_cache = jnp.exp(score_cache - highest_score[..., None])
        weight_draft = jnp.exp(score_draft - highest_score[..., None])
        totals = lax.optimization_barrier(jnp.sum(weight_cache, axis=2)) + lax.optimization_barrier(jnp.sum(weight_draft, axis=2))
        weight_cache = lax.optimization_barrier(weight_cache.astype(jnp.bfloat16)).astype(jnp.float32)
        weight_draft = lax.optimization_barrier(weight_draft.astype(jnp.bfloat16)).astype(jnp.float32)
        mixed_latent = jnp.einsum('ths,sl->thl', weight_cache, cached[:, :LAT])
        mixed_latent = mixed_latent + jnp.einsum('ths,sl->thl', weight_draft, draft_keys[:, :LAT])
        head_out = jnp.einsum('thl,hlv->thv', mixed_latent / totals[..., None], value_weight, precision=highest)
        return head_out.astype(jnp.bfloat16).reshape(DRAFT, H * V_HEAD)
    head_rows = lax.map(one_request, (global_pages, cache_len, ancestry, queries.reshape(REQUESTS, DRAFT, H, QK_NOPE + ROPE), draft_latent.reshape(REQUESTS, DRAFT, KV)))
    head_rows = head_rows.reshape(TOKENS, H * V_HEAD)
    attention = jnp.dot(head_rows, out_proj, preferred_element_type=jnp.float32)
    resid = (hidden_in.astype(jnp.float32) + attention).astype(jnp.bfloat16)
    resid_wide = resid.astype(jnp.float32)
    normed = resid_wide * lax.rsqrt(lax.optimization_barrier(jnp.mean(resid_wide * resid_wide, axis=1, keepdims=True)) + 1e-06)
    normed = (normed * norm_gain.astype(jnp.float32)[None, :]).astype(jnp.bfloat16)
    logits = jnp.dot(normed, router, preferred_element_type=jnp.float32)
    lifted = jax.nn.sigmoid(jnp.take_along_axis(logits, expert_ids, axis=1))
    gates = lifted / lax.optimization_barrier(jnp.sum(lifted, axis=1, keepdims=True))
    shared_gate = jnp.dot(normed, shared_gate_up[0], preferred_element_type=jnp.float32)
    shared_lift = jnp.dot(normed, shared_gate_up[1], preferred_element_type=jnp.float32)
    shared_hidden = (jax.nn.silu(shared_gate) * shared_lift).astype(jnp.bfloat16)
    shared_part = jnp.dot(shared_hidden, shared_down, preferred_element_type=jnp.float32)
    pair_experts = expert_ids.reshape(N_EP, TOK_EP * TOPK)
    marks = (pair_experts[:, :, None] == jnp.arange(EXPERTS, dtype=jnp.int32)[None, None, :]).astype(jnp.int32)
    slot_of = lax.optimization_barrier(jnp.sum(jnp.cumsum(marks, axis=1) * marks, axis=2)) - 1
    group_ids = jnp.arange(N_EP, dtype=jnp.int32)
    placement = (pair_experts * N_EP + group_ids[:, None]) * CAP + slot_of
    pair_token = group_ids[:, None] * TOK_EP + jnp.arange(TOK_EP * TOPK, dtype=jnp.int32)[None, :] // TOPK
    source = jnp.full((EXPERTS * N_EP * CAP,), TOKENS, dtype=jnp.int32).at[placement.reshape(-1)].set(pair_token.reshape(-1))
    padded = jnp.concatenate([normed, jnp.zeros((1, D), jnp.bfloat16)], axis=0)

    def one_expert(expert_items):
        row_index, gate_up, down_weight = expert_items
        rows_in = padded[row_index]
        gate_value = jnp.dot(rows_in, gate_up[0], preferred_element_type=jnp.float32)
        lift_value = jnp.dot(rows_in, gate_up[1], preferred_element_type=jnp.float32)
        hidden_rows = (jax.nn.silu(gate_value) * lift_value).astype(jnp.bfloat16)
        return jnp.dot(hidden_rows, down_weight, preferred_element_type=jnp.float32)
    expert_rows = lax.map(one_expert, (source.reshape(EXPERTS, N_EP * CAP), expert_gate_up, expert_down))
    expert_rows = expert_rows.reshape(EXPERTS * N_EP * CAP, D)
    token_place = placement.reshape(TOKENS, TOPK)
    routed = jnp.zeros((TOKENS, D), jnp.float32)
    for rank in range(TOPK):
        routed = routed + gates[:, rank:rank + 1] * expert_rows[token_place[:, rank]]
    layer_out = (resid_wide + shared_part + routed).astype(jnp.bfloat16)
    starts = cache_len // PAGE
    accepted = ancestry[jnp.arange(REQUESTS, dtype=jnp.int32), accept_leaf]
    own_latent = draft_latent.reshape(REQUESTS, DRAFT, KV).astype(jnp.float32)
    pieces = []
    for req_pos in range(N_REQ):
        page_now = starts + (req_pos - starts) % N_REQ
        slot_now = jnp.take_along_axis(global_pages, page_now[:, None], axis=1)[:, 0]
        old_page = cache_pool[slot_now].astype(jnp.float32)
        offsets = (page_now[:, None] * PAGE + jnp.arange(PAGE, dtype=jnp.int32)[None, :] - cache_len[:, None]).astype(jnp.float32)
        select = accepted[:, None, :] * (depths[:, None, :] == offsets[:, :, None]).astype(jnp.float32)
        written = jnp.einsum('rod,rdk->rok', select, own_latent, precision=highest)
        touched = lax.optimization_barrier(jnp.sum(select, axis=2)) > 0.5
        pieces.append(jnp.where(touched[..., None], written, old_page).astype(jnp.bfloat16))
    new_pages = jnp.stack(pieces, axis=1)
    return (layer_out, new_pages)
```

```python
import math

import jax
import jax.numpy as jnp
from jax import lax
from jax.sharding import PartitionSpec as P

NEGATIVE = -1e30


def ancestors(parents):
    draft_count = parents.shape[-1]
    draft_index = jnp.arange(draft_count, dtype=jnp.int32)
    ancestry = (parents[:, :, None] == draft_index[None, None, :]).astype(jnp.float32)
    ancestry = ancestry + jnp.eye(draft_count, dtype=jnp.float32)[None]
    for doubling in range(max(1, (draft_count - 1).bit_length())):
        ancestry = jnp.minimum(
            jnp.einsum("rij,rjk->rik", ancestry, ancestry, precision=lax.Precision.HIGHEST), 1.0
        )
    return ancestry


def per_device(
    queries,
    draft_latent,
    hidden_in,
    cache_pool,
    page_table,
    cache_len,
    parents,
    accept_leaf,
    absorb_key,
    absorb_value,
    out_proj,
    norm_gain,
    router,
    expert_ids,
    expert_gate_up,
    expert_down,
    shared_gate_up,
    shared_down,
):
    req_count = lax.axis_size("req")
    req_index = lax.axis_index("req")
    ep_count = lax.axis_size("ep")
    request_count, draft_count = parents.shape
    token_count = request_count * draft_count
    head_count = queries.shape[1]
    nope_width = absorb_key.shape[1]
    latent_width = absorb_key.shape[2]
    page_size = cache_pool.shape[1]
    key_width = cache_pool.shape[2]
    page_count = page_table.shape[1]
    score_scale = 1.0 / math.sqrt(queries.shape[2])
    ancestry = ancestors(parents)
    depths = jnp.sum(ancestry, axis=2) - 1.0
    local_pages = page_count // req_count
    page_cols = req_index + req_count * jnp.arange(local_pages, dtype=jnp.int32)
    slot_rows = jnp.take(page_table, page_cols, axis=1)
    cached = cache_pool[slot_rows].reshape(request_count, local_pages * page_size, key_width)
    positions = (
        page_cols[:, None] * page_size + jnp.arange(page_size, dtype=jnp.int32)[None, :]
    ).reshape(-1)
    cache_ok = positions[None, :] < cache_len[:, None]
    draft_share = draft_count // req_count
    draft_cols = req_index * draft_share + jnp.arange(draft_share, dtype=jnp.int32)
    own_latent = draft_latent.reshape(request_count, draft_count, key_width)
    draft_keys = jnp.take(own_latent, draft_cols, axis=1)
    tree_ok = jnp.take(ancestry, draft_cols, axis=2) > 0.5
    absorbed = jnp.einsum(
        "thd,hdl->thl", queries[:, :, :nope_width], absorb_key, preferred_element_type=jnp.float32
    ).astype(jnp.bfloat16)
    query_full = jnp.concatenate([absorbed, queries[:, :, nope_width:]], axis=2)
    query_full = query_full.reshape(request_count, draft_count, head_count, key_width)
    score_cache = (
        jnp.einsum("rthk,rsk->rths", query_full, cached, preferred_element_type=jnp.float32)
        * score_scale
    )
    score_cache = jnp.where(cache_ok[:, None, None, :], score_cache, NEGATIVE)
    score_draft = (
        jnp.einsum("rthk,rsk->rths", query_full, draft_keys, preferred_element_type=jnp.float32)
        * score_scale
    )
    score_draft = jnp.where(tree_ok[:, :, None, :], score_draft, NEGATIVE)
    highest_score = jnp.maximum(jnp.max(score_cache, axis=3), jnp.max(score_draft, axis=3))
    weight_cache = jnp.where(
        cache_ok[:, None, None, :], jnp.exp(score_cache - highest_score[..., None]), 0.0
    )
    weight_draft = jnp.where(
        tree_ok[:, :, None, :], jnp.exp(score_draft - highest_score[..., None]), 0.0
    )
    totals = jnp.sum(weight_cache, axis=3) + jnp.sum(weight_draft, axis=3)
    mixed_latent = jnp.einsum(
        "rths,rsl->rthl",
        weight_cache.astype(jnp.bfloat16),
        cached[:, :, :latent_width],
        preferred_element_type=jnp.float32,
    )
    mixed_latent = mixed_latent + jnp.einsum(
        "rths,rsl->rthl",
        weight_draft.astype(jnp.bfloat16),
        draft_keys[:, :, :latent_width],
        preferred_element_type=jnp.float32,
    )
    projected = jnp.einsum(
        "rthl,hlv->rthv",
        mixed_latent.astype(jnp.bfloat16),
        absorb_value,
        preferred_element_type=jnp.float32,
    ).astype(jnp.bfloat16)
    stats = lax.all_gather(jnp.stack([highest_score, totals]), "req")
    parts = lax.all_gather(projected, "req").astype(jnp.float32)
    factors = jnp.exp(stats[:, 0] - jnp.max(stats[:, 0], axis=0)[None])
    factors = factors / jnp.sum(factors * stats[:, 1], axis=0)[None]
    head_out = jnp.sum(parts * factors[..., None], axis=0)
    head_rows = head_out.astype(jnp.bfloat16).reshape(token_count, -1)
    attention = jnp.dot(head_rows, out_proj, preferred_element_type=jnp.float32)
    resid_cols = (hidden_in.astype(jnp.float32) + attention).astype(jnp.bfloat16)
    resid = lax.all_gather(resid_cols, "req", axis=1, tiled=True)
    resid_wide = resid.astype(jnp.float32)
    normed = resid_wide * lax.rsqrt(
        jnp.mean(resid_wide * resid_wide, axis=1, keepdims=True) + 1e-06
    )
    normed = (normed * norm_gain[None, :]).astype(jnp.bfloat16)
    everyone = lax.all_gather(normed, "ep", axis=0, tiled=True)
    local_experts = expert_gate_up.shape[0]
    expert_total = local_experts * ep_count
    named = jnp.any(
        expert_ids[:, :, None] == jnp.arange(expert_total, dtype=jnp.int32)[None, None, :], axis=1
    ).astype(jnp.float32)
    logits = jnp.dot(normed, router, preferred_element_type=jnp.float32)
    lifted = jax.nn.sigmoid(logits) * named
    gates = lifted / jnp.sum(lifted, axis=1, keepdims=True)
    gates_all = lax.all_gather(gates, "ep", axis=0, tiled=True)
    own_gates = lax.dynamic_slice_in_dim(
        gates_all, lax.axis_index("ep") * local_experts, local_experts, axis=1
    )
    shared_gate = jnp.dot(normed, shared_gate_up[0], preferred_element_type=jnp.float32)
    shared_lift = jnp.dot(normed, shared_gate_up[1], preferred_element_type=jnp.float32)
    shared_hidden = (jax.nn.silu(shared_gate) * shared_lift).astype(jnp.bfloat16)
    shared_part = jnp.dot(shared_hidden, shared_down, preferred_element_type=jnp.float32)
    term = 0.0
    for e in range(local_experts):
        gate_value = jnp.dot(
            everyone, expert_gate_up[e, 0], preferred_element_type=jnp.float32
        )
        lift_value = jnp.dot(
            everyone, expert_gate_up[e, 1], preferred_element_type=jnp.float32
        )
        hidden_rows = (jax.nn.silu(gate_value) * lift_value).astype(jnp.bfloat16)
        result = jnp.dot(hidden_rows, expert_down[e], preferred_element_type=jnp.float32)
        term = term + own_gates[:, e : e + 1] * result
    routed = lax.psum_scatter(
        term.astype(jnp.bfloat16), "ep", scatter_dimension=0, tiled=True
    ).astype(jnp.float32)
    summed = lax.psum_scatter(
        (shared_part + routed).astype(jnp.bfloat16), "req", scatter_dimension=1, tiled=True
    ).astype(jnp.float32)
    layer_out = (resid_cols.astype(jnp.float32) + summed).astype(jnp.bfloat16)
    starts = cache_len // page_size
    page_now = starts + jnp.mod(req_index - starts, req_count)
    slot_now = jnp.take_along_axis(page_table, page_now[:, None], axis=1)[:, 0]
    old_page = cache_pool[slot_now]
    offsets = (
        page_now[:, None] * page_size
        + jnp.arange(page_size, dtype=jnp.int32)[None, :]
        - cache_len[:, None]
    ).astype(jnp.float32)
    accepted = jnp.take_along_axis(ancestry, accept_leaf[:, None, None], axis=1)[:, 0, :]
    select = accepted[:, None, :] * (depths[:, None, :] == offsets[:, :, None]).astype(jnp.float32)
    written = jnp.einsum(
        "rod,rdk->rok", select.astype(jnp.bfloat16), own_latent, preferred_element_type=jnp.float32
    )
    touched = jnp.sum(select, axis=2) > 0.5
    fresh = jnp.where(touched[..., None], written, old_page.astype(jnp.float32)).astype(
        jnp.bfloat16
    )
    return (layer_out, fresh[:, None])


def solution(mesh):
    in_specs = (
        P("ep", None, None),
        P("ep", None),
        P("ep", "req"),
        P(("req", "ep"), None, None),
        P("ep", None),
        P("ep"),
        P("ep", None),
        P("ep"),
        P(),
        P(),
        P(None, "req"),
        P(),
        P(),
        P("ep", None),
        P("ep", None, None, "req"),
        P("ep", "req", None),
        P(None, None, "req"),
        P("req", None),
    )
    out_specs = (P("ep", "req"), P("ep", "req", None, None))
    return jax.shard_map(
        per_device, mesh=mesh, in_specs=in_specs, out_specs=out_specs, check_vma=False
    )
```

```python
import functools
import math

import jax
import jax.numpy as jnp
from jax import lax
from jax.experimental import pallas as pl
from jax.experimental.pallas import tpu as pltpu
from jax.sharding import PartitionSpec as P

NEGATIVE = -1e30
FLOOR = -1e29
MESH = pl.DeviceIdType.MESH


DRAFT_PAD = 128


def attend_kernel(scale, page_count, slots, absorbed, rotary, *rest):
    pages = rest[:page_count]
    drafts, cache_bias, tree_bias, value, projected, peaks, sums, keys, bias = rest[page_count:]
    page_size = pages[0].shape[1]
    cached = page_count * page_size
    draft_count = drafts.shape[1]
    latent_width = absorbed.shape[2]
    head_count = absorbed.shape[0]
    group = head_count // projected.shape[0]
    value_width = value.shape[2]
    for p in range(page_count):
        keys[p * page_size : (p + 1) * page_size, :] = pages[p][0]
    keys[cached : cached + draft_count, :] = drafts[0]
    keys[cached + draft_count :, :] = jnp.zeros(
        (DRAFT_PAD - draft_count, keys.shape[1]), keys.dtype
    )
    bias[:, :cached] = jnp.broadcast_to(cache_bias[0], (draft_count, cached))
    bias[:, cached:] = tree_bias[0]
    contract_last = (((1,), (1,)), ((), ()))
    peaks[...] = jnp.zeros_like(peaks)
    sums[...] = jnp.ones_like(sums)

    for chunk in range(head_count // group):
        rows = slice(chunk * group, (chunk + 1) * group)
        nope = absorbed[rows].reshape(group * draft_count, latent_width)
        rope = rotary[rows].reshape(group * draft_count, rotary.shape[2])
        scores = lax.dot_general(
            nope, keys[:, :latent_width], contract_last, preferred_element_type=jnp.float32
        ) + lax.dot_general(
            rope, keys[:, latent_width:], contract_last, preferred_element_type=jnp.float32
        )
        scores = scores.reshape(group, draft_count, -1) * scale + bias[...][None]
        scores = scores.reshape(group * draft_count, -1)
        peak = jnp.maximum(jnp.max(scores, axis=1, keepdims=True), FLOOR)
        weights = jnp.exp(scores - peak)
        total = jnp.sum(weights, axis=1, keepdims=True)
        mixed = jnp.dot(
            weights.astype(jnp.bfloat16), keys[:, :latent_width],
            preferred_element_type=jnp.float32,
        ).astype(jnp.bfloat16)
        for j in range(group):
            h = chunk * group + j
            own = slice(j * draft_count, (j + 1) * draft_count)
            projected[chunk, :, j * value_width : (j + 1) * value_width] = jnp.dot(
                mixed[own], value[h], preferred_element_type=jnp.float32
            ).astype(jnp.bfloat16)
            peaks[:, h : h + 1] = peak[own]
            sums[:, h : h + 1] = total[own]


def attend(slots, absorbed, rotary, pool, drafts, cache_bias, tree_bias, value, scale, chunks):
    requests, page_count = slots.shape
    heads, tokens, latent_width = absorbed.shape
    page_size, key_width = pool.shape[1:]
    draft_count = drafts.shape[1]
    width = heads // chunks * value.shape[2]
    cached = page_count * page_size

    def page_spec(p):
        return pl.BlockSpec((1, page_size, key_width), lambda r, table: (table[r, p], 0, 0))

    def by_request(shape):
        return pl.BlockSpec((1,) + shape, lambda r, table: (r, 0, 0))

    return pl.pallas_call(
        functools.partial(attend_kernel, scale, page_count),
        grid_spec=pltpu.PrefetchScalarGridSpec(
            num_scalar_prefetch=1,
            grid=(requests,),
            in_specs=[
                pl.BlockSpec((heads, draft_count, latent_width), lambda r, table: (0, r, 0)),
                pl.BlockSpec((heads, draft_count, rotary.shape[2]), lambda r, table: (0, r, 0)),
                *[page_spec(p) for p in range(page_count)],
                by_request((draft_count, key_width)),
                by_request((1, cached)),
                by_request((draft_count, DRAFT_PAD)),
                pl.BlockSpec(value.shape, lambda r, table: (0, 0, 0)),
            ],
            out_specs=[
                pl.BlockSpec((chunks, draft_count, width), lambda r, table: (0, r, 0)),
                pl.BlockSpec((draft_count, 128), lambda r, table: (r, 0)),
                pl.BlockSpec((draft_count, 128), lambda r, table: (r, 0)),
            ],
            scratch_shapes=[
                pltpu.VMEM((cached + DRAFT_PAD, key_width), jnp.bfloat16),
                pltpu.VMEM((draft_count, cached + DRAFT_PAD), jnp.float32),
            ],
        ),
        out_shape=[
            jax.ShapeDtypeStruct((chunks, tokens, width), jnp.bfloat16),
            jax.ShapeDtypeStruct((tokens, 128), jnp.float32),
            jax.ShapeDtypeStruct((tokens, 128), jnp.float32),
        ],
        compiler_params=pltpu.CompilerParams(vmem_limit_bytes=40 * 1024 * 1024),
    )(slots, absorbed, rotary, *[pool] * page_count, drafts, cache_bias, tree_bias, value)


def exchange_kernel(
    n_req, n_ep, parts, stats, hidden, out_proj_hbm, gain, router, named, gate_up_hbm, down_hbm,
    shared_up_hbm, shared_down_hbm, out,
    out_proj, gate_up, down, shared_up, shared_down, weight_sem,
    part_in, stat_in, head_in, resid_in, final_out, final_in, z_send, z_recv,
    rows, gates, mate_out, mate_in, back_out, back_in, total,
    row_send, row_recv, fwd_send, fwd_recv, mate_send, mate_recv, back_send, back_recv,
):
    f32, bf16 = jnp.float32, jnp.bfloat16
    req = lax.axis_index("req")
    ep = lax.axis_index("ep")
    chips = n_ep // 2
    core = ep % 2
    chip = ep // 2
    mate = chip * 2 + 1 - core
    tokens, width = hidden.shape
    group = stats.shape[1] // 2
    value_width = width // group
    expert_total = named.shape[1]
    local_experts = gate_up.shape[0]

    def partner(s):
        there, bit = 0, 1
        while bit < chips:
            there = there + bit * (((chip // bit) % 2 + (s // bit) % 2) % 2)
            bit *= 2
        return there * 2 + core

    loads = [
        pltpu.make_async_copy(src, dst, weight_sem.at[i])
        for i, (src, dst) in enumerate(
            [
                (out_proj_hbm, out_proj),
                (shared_up_hbm, shared_up),
                (shared_down_hbm, shared_down),
                (gate_up_hbm, gate_up),
                (down_hbm, down),
            ]
        )
    ]
    for load in loads:
        load.start()

    barrier = pltpu.get_barrier_semaphore()
    for delta in range(1, n_req):
        pl.semaphore_signal(
            barrier, inc=1, device_id=((req + delta) % n_req, ep), device_id_type=MESH
        )
    for s in range(1, chips):
        pl.semaphore_signal(barrier, inc=1, device_id=(req, partner(s)), device_id_type=MESH)
    pl.semaphore_signal(barrier, inc=1, device_id=(req, mate), device_id_type=MESH)
    pl.semaphore_wait(barrier, n_req - 1 + chips)

    def along_z(stage, delta, src, dst):
        return pltpu.make_async_remote_copy(
            src_ref=src, dst_ref=dst,
            send_sem=z_send.at[stage, delta], recv_sem=z_recv.at[stage, delta],
            device_id=((req + delta) % n_req, ep), device_id_type=MESH,
        )

    sent = []
    for delta in range(1, n_req):
        to = (req + delta) % n_req
        sent.append(along_z(0, delta, parts.at[to], part_in.at[delta]))
        sent.append(along_z(1, delta, stats.at[to], stat_in.at[delta]))
    for copy in sent:
        copy.start()
    part_in[0] = parts[req]
    stat_in[0] = stats[req]
    for copy in sent:
        copy.wait()

    flat = stat_in[...].reshape(n_req * 2 * group, tokens)
    flat = jnp.concatenate([flat, jnp.zeros((128 - flat.shape[0], tokens), f32)], axis=0)
    columns = flat.T
    for j in range(group):
        at = [d * 2 * group + j for d in range(n_req)]
        peak = [columns[:, i : i + 1] for i in at]
        total_at = [columns[:, i + group : i + group + 1] for i in at]
        top = functools.reduce(jnp.maximum, peak)
        factor = [jnp.exp(p - top) for p in peak]
        inverse = 1.0 / sum(f * t for f, t in zip(factor, total_at))
        lanes = slice(j * value_width, (j + 1) * value_width)
        head = sum(
            part_in[d, :, lanes].astype(f32) * (factor[d] * inverse) for d in range(n_req)
        )
        head_in[0, :, lanes] = head.astype(bf16)

    sent = [along_z(2, d, head_in.at[0], head_in.at[d]) for d in range(1, n_req)]
    for copy in sent:
        copy.start()
    loads[0].wait()

    def project(delta):
        src = (req + n_req - delta) % n_req
        return jnp.dot(
            head_in[delta], out_proj[pl.ds(pl.multiple_of(src * width, width), width), :],
            preferred_element_type=f32,
        )

    attention = project(0)
    for d in range(1, n_req):
        sent[d - 1].wait()
        attention = attention + project(d)
    own_resid = (hidden[...].astype(f32) + attention).astype(bf16)
    resid_in[req] = own_resid
    sent = [along_z(3, d, resid_in.at[req], resid_in.at[req]) for d in range(1, n_req)]
    for copy in sent:
        copy.start()
    for copy in sent:
        copy.wait()

    square = 0.0
    for d in range(n_req):
        wide = resid_in[d].astype(f32)
        square = square + jnp.sum(wide * wide, axis=1, keepdims=True)
    inverse = lax.rsqrt(square / (n_req * width) + 1e-06)
    for d in range(n_req):
        lanes = slice(d * width, (d + 1) * width)
        rows[0, 0, :, lanes] = (
            resid_in[d].astype(f32) * inverse * gain[:, lanes]
        ).astype(bf16)
    logits = jnp.dot(rows[0, 0], router[...], preferred_element_type=f32)
    lifted = named[...] / (1.0 + jnp.exp(-logits))
    gate = lifted / jnp.sum(lifted, axis=1, keepdims=True)
    gate = jnp.concatenate([gate, jnp.zeros((tokens, 128 - expert_total), f32)], axis=1)
    gates[0, 0] = gate.T[:expert_total]

    def spread(s):
        to = (req, partner(s))
        return [
            pltpu.make_async_remote_copy(
                src_ref=buf.at[0, 0], dst_ref=buf.at[s, 0],
                send_sem=row_send.at[s, i], recv_sem=row_recv.at[s, i],
                device_id=to, device_id_type=MESH,
            )
            for i, buf in enumerate((rows, gates))
        ]

    def forward(s):
        return [
            pltpu.make_async_remote_copy(
                src_ref=buf.at[s, 0], dst_ref=buf.at[s, 1],
                send_sem=fwd_send.at[s, i], recv_sem=fwd_recv.at[s, i],
                device_id=(req, mate), device_id_type=MESH,
            )
            for i, buf in enumerate((rows, gates))
        ]

    def to_mate(s):
        return pltpu.make_async_remote_copy(
            src_ref=mate_out.at[s], dst_ref=mate_in.at[s],
            send_sem=mate_send.at[s], recv_sem=mate_recv.at[s],
            device_id=(req, mate), device_id_type=MESH,
        )

    def send_back(s):
        return pltpu.make_async_remote_copy(
            src_ref=back_out.at[s], dst_ref=back_in.at[s],
            send_sem=back_send.at[s], recv_sem=back_recv.at[s],
            device_id=(req, partner(s)), device_id_type=MESH,
        )

    for s in range(1, chips):
        for copy in spread(s):
            copy.start()
    for copy in forward(0):
        copy.start()

    def silu_times(value, lift):
        return value / (1.0 + jnp.exp(-value)) * lift

    loads[1].wait()
    loads[2].wait()
    shared_hidden = silu_times(
        jnp.dot(rows[0, 0], shared_up[0], preferred_element_type=f32),
        jnp.dot(rows[0, 0], shared_up[1], preferred_element_type=f32),
    ).astype(bf16)
    total[...] = jnp.dot(shared_hidden, shared_down[...], preferred_element_type=f32)
    loads[3].wait()
    loads[4].wait()

    def step(s, carry):
        @pl.when(s > 0)
        def _():
            for copy in spread(s):
                copy.wait_recv()
            for copy in forward(s):
                copy.start()

        for copy in forward(s):
            copy.wait_recv()
        both = rows[s].reshape(2 * tokens, n_req * width)
        own_gate = []
        for k in range(2):
            flat = gates[s, k]
            flat = jnp.concatenate([flat, jnp.zeros((128 - expert_total, tokens), f32)], axis=0)
            own_gate.append(flat.T)
        own_gate = jnp.concatenate(own_gate, axis=0)
        lane = lax.broadcasted_iota(jnp.int32, own_gate.shape, 1)
        weighted = []
        for e in range(local_experts):
            column = jnp.sum(
                jnp.where(lane == ep * local_experts + e, own_gate, 0.0), axis=1, keepdims=True
            )
            hidden_rows = silu_times(
                jnp.dot(both, gate_up[e, 0], preferred_element_type=f32),
                jnp.dot(both, gate_up[e, 1], preferred_element_type=f32),
            )
            weighted.append((hidden_rows * column).astype(bf16))

        def result(k):
            return sum(
                jnp.dot(
                    weighted[e][k * tokens : (k + 1) * tokens], down[e],
                    preferred_element_type=f32,
                )
                for e in range(local_experts)
            )

        mate_out[s] = result(1).astype(bf16)
        to_mate(s).start()
        own = result(0)
        to_mate(s).wait_recv()
        own = own + mate_in[s].astype(f32)

        @pl.when(s == 0)
        def _():
            total[...] += own

        @pl.when(s > 0)
        def _():
            back_out[s] = own.astype(bf16)
            send_back(s).start()

        return carry

    lax.fori_loop(0, chips, step, 0)
    summed = total[...]
    for s in range(1, chips):
        send_back(s).wait_recv()
        summed = summed + back_in[s].astype(f32)
    total[...] = summed
    for d in range(n_req):
        final_out[d] = summed[:, d * width : (d + 1) * width].astype(bf16)
    sent = []
    for delta in range(1, n_req):
        to = (req + delta) % n_req
        sent.append(along_z(4, delta, final_out.at[to], final_in.at[delta]))
    for copy in sent:
        copy.start()
    for s in range(chips):
        for copy in forward(s):
            copy.wait_send()
        to_mate(s).wait_send()
        if s:
            for copy in spread(s):
                copy.wait_send()
            send_back(s).wait_send()
    answer = resid_in[req].astype(f32) + final_out[req].astype(f32)
    for d in range(1, n_req):
        sent[d - 1].wait()
        answer = answer + final_in[d].astype(f32)
    out[...] = answer.astype(bf16)


def exchange(
    parts, stats, hidden, out_proj, gain, router, named, gate_up, down, shared_up, shared_down,
    n_req, n_ep,
):
    tokens, width = hidden.shape
    model = n_req * width
    chips = n_ep // 2
    bf16, f32 = jnp.bfloat16, jnp.float32
    in_vmem = pl.BlockSpec(memory_space=pltpu.VMEM)
    in_any = pl.BlockSpec(memory_space=pl.ANY)
    dma = pltpu.SemaphoreType.DMA
    weights = [out_proj, gate_up, down, shared_up, shared_down]
    return pl.pallas_call(
        functools.partial(exchange_kernel, n_req, n_ep),
        out_shape=jax.ShapeDtypeStruct((tokens, width), bf16),
        in_specs=[in_vmem] * 3 + [in_any] + [in_vmem] * 3 + [in_any] * 4,
        out_specs=in_vmem,
        scratch_shapes=[
            *[pltpu.VMEM(w.shape, w.dtype) for w in weights],
            dma((5,)),
            pltpu.VMEM(parts.shape, bf16),
            pltpu.VMEM(stats.shape, f32),
            pltpu.VMEM((n_req, tokens, width), bf16),
            pltpu.VMEM((n_req, tokens, width), bf16),
            pltpu.VMEM((n_req, tokens, width), bf16),
            pltpu.VMEM((n_req, tokens, width), bf16),
            dma((5, n_req)),
            dma((5, n_req)),
            pltpu.VMEM((chips, 2, tokens, model), bf16),
            pltpu.VMEM((chips, 2, named.shape[1], tokens), f32),
            pltpu.VMEM((chips, tokens, model), bf16),
            pltpu.VMEM((chips, tokens, model), bf16),
            pltpu.VMEM((chips, tokens, model), bf16),
            pltpu.VMEM((chips, tokens, model), bf16),
            pltpu.VMEM((tokens, model), f32),
            dma((chips, 2)),
            dma((chips, 2)),
            dma((chips, 2)),
            dma((chips, 2)),
            dma((chips,)),
            dma((chips,)),
            dma((chips,)),
            dma((chips,)),
        ],
        compiler_params=pltpu.CompilerParams(
            collective_id=0, has_side_effects=True, vmem_limit_bytes=56 * 1024 * 1024
        ),
    )(parts, stats, hidden, out_proj, gain, router, named, gate_up, down, shared_up, shared_down)


def ancestors(parents):
    draft_count = parents.shape[-1]
    draft_index = jnp.arange(draft_count, dtype=jnp.int32)
    ancestry = (parents[:, :, None] == draft_index[None, None, :]).astype(jnp.float32)
    ancestry = ancestry + jnp.eye(draft_count, dtype=jnp.float32)[None]
    for doubling in range(max(1, (draft_count - 1).bit_length())):
        ancestry = jnp.minimum(
            jnp.einsum("rij,rjk->rik", ancestry, ancestry, precision=lax.Precision.HIGHEST), 1.0
        )
    return ancestry


def per_device(
    queries,
    draft_latent,
    hidden_in,
    cache_pool,
    page_table,
    cache_len,
    parents,
    accept_leaf,
    absorb_key,
    absorb_value,
    out_proj,
    norm_gain,
    router,
    expert_ids,
    expert_gate_up,
    expert_down,
    shared_gate_up,
    shared_down,
):
    req_count = lax.axis_size("req")
    req_index = lax.axis_index("req")
    ep_count = lax.axis_size("ep")
    request_count, draft_count = parents.shape
    token_count = request_count * draft_count
    head_count = queries.shape[1]
    nope_width = absorb_key.shape[1]
    latent_width = absorb_key.shape[2]
    page_size = cache_pool.shape[1]
    key_width = cache_pool.shape[2]
    page_count = page_table.shape[1]
    score_scale = 1.0 / math.sqrt(queries.shape[2])
    ancestry = ancestors(parents)
    depths = jnp.sum(ancestry, axis=2) - 1.0
    local_pages = page_count // req_count
    page_cols = req_index + req_count * jnp.arange(local_pages, dtype=jnp.int32)
    slot_rows = jnp.take(page_table, page_cols, axis=1)
    positions = (
        page_cols[:, None] * page_size + jnp.arange(page_size, dtype=jnp.int32)[None, :]
    ).reshape(-1)
    cache_bias = jnp.where(positions[None, :] < cache_len[:, None], 0.0, NEGATIVE)[:, None, :]
    draft_share = draft_count // req_count
    draft_index = jnp.arange(draft_count, dtype=jnp.int32)
    own_draft = draft_index // draft_share == req_index
    tree_bias = jnp.where((ancestry > 0.5) & own_draft[None, None, :], 0.0, NEGATIVE)
    tree_bias = jnp.pad(
        tree_bias, ((0, 0), (0, 0), (0, DRAFT_PAD - draft_count)), constant_values=NEGATIVE
    )
    own_latent = draft_latent.reshape(request_count, draft_count, key_width)
    absorbed = jnp.einsum(
        "thd,hdl->htl", queries[:, :, :nope_width], absorb_key, preferred_element_type=jnp.float32
    ).astype(jnp.bfloat16)
    rotary = jnp.transpose(queries[:, :, nope_width:], (1, 0, 2))
    projected, peaks, sums = attend(
        slot_rows, absorbed, rotary, cache_pool, own_latent, cache_bias, tree_bias, absorb_value,
        score_scale, req_count,
    )
    local_experts = expert_gate_up.shape[0]
    expert_total = local_experts * ep_count
    named = jnp.any(
        expert_ids[:, :, None] == jnp.arange(expert_total, dtype=jnp.int32)[None, None, :], axis=1
    ).astype(jnp.float32)
    if ep_count <= 8:
        group = head_count // req_count
        by_head = jnp.stack([peaks[:, :head_count].T, sums[:, :head_count].T])
        by_head = by_head.reshape(2, req_count, group, token_count)
        by_head = jnp.transpose(by_head, (1, 0, 2, 3)).reshape(req_count, 2 * group, token_count)
        layer_out = exchange(
            projected, by_head, hidden_in, out_proj, norm_gain.reshape(1, -1), router, named,
            expert_gate_up, expert_down, shared_gate_up, shared_down, req_count, ep_count,
        )
    else:
        stats = lax.all_gather(jnp.stack([peaks, sums]), "req")
        parts = lax.all_gather(projected, "req").astype(jnp.float32)
        factors = jnp.exp(stats[:, 0] - jnp.max(stats[:, 0], axis=0)[None])
        factors = factors / jnp.sum(factors * stats[:, 1], axis=0)[None]
        factors = jnp.transpose(factors[..., :head_count], (0, 2, 1))
        parts = parts.reshape(req_count, req_count, token_count, head_count // req_count, -1)
        parts = jnp.transpose(parts, (0, 1, 3, 2, 4)).reshape(req_count, head_count, token_count, -1)
        head_out = jnp.transpose(jnp.sum(parts * factors[..., None], axis=0), (1, 0, 2))
        head_rows = head_out.astype(jnp.bfloat16).reshape(token_count, -1)
        attention = jnp.dot(head_rows, out_proj, preferred_element_type=jnp.float32)
        resid_cols = (hidden_in.astype(jnp.float32) + attention).astype(jnp.bfloat16)
        resid = lax.all_gather(resid_cols, "req", axis=1, tiled=True)
        resid_wide = resid.astype(jnp.float32)
        normed = resid_wide * lax.rsqrt(
            jnp.mean(resid_wide * resid_wide, axis=1, keepdims=True) + 1e-06
        )
        normed = (normed * norm_gain[None, :]).astype(jnp.bfloat16)
        everyone = lax.all_gather(normed, "ep", axis=0, tiled=True)
        logits = jnp.dot(normed, router, preferred_element_type=jnp.float32)
        lifted = jax.nn.sigmoid(logits) * named
        gates = lifted / jnp.sum(lifted, axis=1, keepdims=True)
        gates_all = lax.all_gather(gates, "ep", axis=0, tiled=True)
        own_gates = lax.dynamic_slice_in_dim(
            gates_all, lax.axis_index("ep") * local_experts, local_experts, axis=1
        )
        shared_gate = jnp.dot(normed, shared_gate_up[0], preferred_element_type=jnp.float32)
        shared_lift = jnp.dot(normed, shared_gate_up[1], preferred_element_type=jnp.float32)
        shared_hidden = (jax.nn.silu(shared_gate) * shared_lift).astype(jnp.bfloat16)
        shared_part = jnp.dot(shared_hidden, shared_down, preferred_element_type=jnp.float32)
        term = 0.0
        for e in range(local_experts):
            gate_value = jnp.dot(
                everyone, expert_gate_up[e, 0], preferred_element_type=jnp.float32
            )
            lift_value = jnp.dot(
                everyone, expert_gate_up[e, 1], preferred_element_type=jnp.float32
            )
            hidden_rows = (jax.nn.silu(gate_value) * lift_value).astype(jnp.bfloat16)
            result = jnp.dot(hidden_rows, expert_down[e], preferred_element_type=jnp.float32)
            term = term + own_gates[:, e : e + 1] * result
        routed = lax.psum_scatter(
            term.astype(jnp.bfloat16), "ep", scatter_dimension=0, tiled=True
        ).astype(jnp.float32)
        summed = lax.psum_scatter(
            (shared_part + routed).astype(jnp.bfloat16), "req", scatter_dimension=1, tiled=True
        ).astype(jnp.float32)
        layer_out = (resid_cols.astype(jnp.float32) + summed).astype(jnp.bfloat16)
    starts = cache_len // page_size
    page_now = starts + jnp.mod(req_index - starts, req_count)
    slot_now = jnp.take_along_axis(page_table, page_now[:, None], axis=1)[:, 0]
    old_page = cache_pool[slot_now]
    offsets = (
        page_now[:, None] * page_size
        + jnp.arange(page_size, dtype=jnp.int32)[None, :]
        - cache_len[:, None]
    ).astype(jnp.float32)
    accepted = jnp.take_along_axis(ancestry, accept_leaf[:, None, None], axis=1)[:, 0, :]
    select = accepted[:, None, :] * (depths[:, None, :] == offsets[:, :, None]).astype(jnp.float32)
    written = jnp.einsum(
        "rod,rdk->rok", select.astype(jnp.bfloat16), own_latent, preferred_element_type=jnp.float32
    )
    touched = jnp.sum(select, axis=2) > 0.5
    fresh = jnp.where(touched[..., None], written, old_page.astype(jnp.float32)).astype(
        jnp.bfloat16
    )
    return (layer_out, fresh[:, None])


def solution(mesh):
    in_specs = (
        P("ep", None, None),
        P("ep", None),
        P("ep", "req"),
        P(("req", "ep"), None, None),
        P("ep", None),
        P("ep"),
        P("ep", None),
        P("ep"),
        P(),
        P(),
        P(None, "req"),
        P(),
        P(),
        P("ep", None),
        P("ep", None, None, "req"),
        P("ep", "req", None),
        P(None, None, "req"),
        P("req", None),
    )
    out_specs = (P("ep", "req"), P("ep", "req", None, None))
    return jax.shard_map(
        per_device, mesh=mesh, in_specs=in_specs, out_specs=out_specs, check_vma=False
    )
```

```python
import functools
import math

import jax
import jax.numpy as jnp
from jax import lax
from jax.experimental import pallas as pl
from jax.experimental.pallas import tpu as pltpu
from jax.sharding import PartitionSpec as P

NEGATIVE = -1e30
FLOOR = -1e29
MESH = pl.DeviceIdType.MESH


def attend_kernel(scale, page_count, slots, absorbed, rotary, *rest):
    pages = rest[:page_count]
    old_page, drafts, cache_bias, tree_bias, value, select, touched = rest[page_count:-6]
    projected, peaks, sums, fresh, keys, bias = rest[-6:]
    page_size = pages[0].shape[2]
    cached = page_count * page_size
    draft_count = tree_bias.shape[1]
    latent_width = absorbed.shape[2]
    head_count = absorbed.shape[0]
    group = head_count // projected.shape[0]
    value_width = value.shape[2]
    for p in range(page_count):
        keys[:, p * page_size : (p + 1) * page_size] = pages[p][0]
    keys[:, cached:] = drafts[...]
    written = jnp.dot(drafts[...], select[0], preferred_element_type=jnp.float32)
    fresh[0] = jnp.where(
        touched[0] > 0.5, written, old_page[0].astype(jnp.float32)
    ).astype(jnp.bfloat16)
    bias[:, :cached] = jnp.broadcast_to(cache_bias[0], (draft_count, cached))
    bias[:, cached:] = tree_bias[0]
    contract_last = (((1,), (1,)), ((), ()))
    peaks[...] = jnp.zeros_like(peaks)
    sums[...] = jnp.ones_like(sums)

    for chunk in range(head_count // group):
        rows = slice(chunk * group, (chunk + 1) * group)
        nope = absorbed[rows].reshape(group * draft_count, latent_width)
        rope = rotary[rows].reshape(group * draft_count, rotary.shape[2])
        scores = jnp.dot(
            nope, keys[:latent_width, :], preferred_element_type=jnp.float32
        ) + jnp.dot(rope, keys[latent_width:, :], preferred_element_type=jnp.float32)
        scores = scores.reshape(group, draft_count, -1) * scale + bias[...][None]
        scores = scores.reshape(group * draft_count, -1)
        peak = jnp.maximum(jnp.max(scores, axis=1, keepdims=True), FLOOR)
        weights = jnp.exp(scores - peak)
        total = jnp.sum(weights, axis=1, keepdims=True)
        mixed = lax.dot_general(
            weights.astype(jnp.bfloat16), keys[:latent_width, :], contract_last,
            preferred_element_type=jnp.float32,
        ).astype(jnp.bfloat16)
        for j in range(group):
            h = chunk * group + j
            own = slice(j * draft_count, (j + 1) * draft_count)
            projected[chunk, :, j * value_width : (j + 1) * value_width] = jnp.dot(
                mixed[own], value[h], preferred_element_type=jnp.float32
            ).astype(jnp.bfloat16)
            peaks[:, h : h + 1] = peak[own]
            sums[:, h : h + 1] = total[own]


def attend(
    slots, absorbed, rotary, pool, drafts, cache_bias, tree_bias, value, select, touched, scale,
    chunks,
):
    requests, page_count = slots.shape[0], slots.shape[1] - 1
    heads, tokens, latent_width = absorbed.shape
    key_width, page_size = pool.shape[1:]
    draft_count = tree_bias.shape[1]
    width = heads // chunks * value.shape[2]
    cached = page_count * page_size

    def page_spec(p):
        return pl.BlockSpec((1, key_width, page_size), lambda r, table: (table[r, p], 0, 0))

    def by_request(shape):
        return pl.BlockSpec((1,) + shape, lambda r, table: (r, 0, 0))

    return pl.pallas_call(
        functools.partial(attend_kernel, scale, page_count),
        grid_spec=pltpu.PrefetchScalarGridSpec(
            num_scalar_prefetch=1,
            grid=(requests,),
            in_specs=[
                pl.BlockSpec((heads, draft_count, latent_width), lambda r, table: (0, r, 0)),
                pl.BlockSpec((heads, draft_count, rotary.shape[2]), lambda r, table: (0, r, 0)),
                *[page_spec(p) for p in range(page_count + 1)],
                pl.BlockSpec(drafts.shape, lambda r, table: (0, 0)),
                by_request((1, cached)),
                by_request((draft_count, tokens)),
                pl.BlockSpec(value.shape, lambda r, table: (0, 0, 0)),
                by_request((tokens, page_size)),
                by_request((1, page_size)),
            ],
            out_specs=[
                pl.BlockSpec((chunks, draft_count, width), lambda r, table: (0, r, 0)),
                pl.BlockSpec((draft_count, 128), lambda r, table: (r, 0)),
                pl.BlockSpec((draft_count, 128), lambda r, table: (r, 0)),
                by_request((key_width, page_size)),
            ],
            scratch_shapes=[
                pltpu.VMEM((key_width, cached + tokens), jnp.bfloat16),
                pltpu.VMEM((draft_count, cached + tokens), jnp.float32),
            ],
        ),
        out_shape=[
            jax.ShapeDtypeStruct((chunks, tokens, width), jnp.bfloat16),
            jax.ShapeDtypeStruct((tokens, 128), jnp.float32),
            jax.ShapeDtypeStruct((tokens, 128), jnp.float32),
            jax.ShapeDtypeStruct((requests, key_width, page_size), jnp.bfloat16),
        ],
        compiler_params=pltpu.CompilerParams(vmem_limit_bytes=58 * 1024 * 1024),
    )(
        slots, absorbed, rotary, *[pool] * (page_count + 1), drafts, cache_bias, tree_bias, value,
        select, touched,
    )


def exchange_kernel(
    n_req, n_ep, parts, stats, hidden, out_proj_hbm, gain, router, named, gate_up_hbm, down_hbm,
    shared_up_hbm, shared_down_hbm, out,
    out_proj, gate_up, down, shared_up, shared_down, weight_sem,
    part_in, stat_in, head_in, resid_in, final_out, final_in, z_send, z_recv,
    rows, gates, mate_out, mate_in, back_out, back_in, total,
    row_send, row_recv, fwd_send, fwd_recv, mate_send, mate_recv, back_send, back_recv,
):
    f32, bf16 = jnp.float32, jnp.bfloat16
    req = lax.axis_index("req")
    ep = lax.axis_index("ep")
    chips = n_ep // 2
    core = ep % 2
    chip = ep // 2
    mate = chip * 2 + 1 - core
    tokens, width = hidden.shape
    group = stats.shape[1] // 2
    value_width = width // group
    expert_total = named.shape[0]
    local_experts = gate_up.shape[0]

    def across(left, right):
        return lax.dot_general(
            left, right, (((1,), (1,)), ((), ())), preferred_element_type=f32
        )

    def partner(s):
        there, bit = 0, 1
        while bit < chips:
            there = there + bit * (((chip // bit) % 2 + (s // bit) % 2) % 2)
            bit *= 2
        return there * 2 + core

    loads = [
        pltpu.make_async_copy(src, dst, weight_sem.at[i])
        for i, (src, dst) in enumerate(
            [
                (out_proj_hbm, out_proj),
                (shared_up_hbm, shared_up),
                (shared_down_hbm, shared_down),
                (gate_up_hbm, gate_up),
                (down_hbm, down),
            ]
        )
    ]
    for load in loads:
        load.start()

    barrier = pltpu.get_barrier_semaphore()
    for delta in range(1, n_req):
        pl.semaphore_signal(
            barrier, inc=1, device_id=((req + delta) % n_req, ep), device_id_type=MESH
        )
    for s in range(1, chips):
        pl.semaphore_signal(barrier, inc=1, device_id=(req, partner(s)), device_id_type=MESH)
    pl.semaphore_signal(barrier, inc=1, device_id=(req, mate), device_id_type=MESH)
    pl.semaphore_wait(barrier, n_req - 1 + chips)

    halves = [slice(0, tokens // 2), slice(tokens // 2, tokens)]

    def along_z(stage, delta, src, dst, half=0):
        return pltpu.make_async_remote_copy(
            src_ref=src, dst_ref=dst,
            send_sem=z_send.at[stage, half, delta], recv_sem=z_recv.at[stage, half, delta],
            device_id=((req + delta) % n_req, ep), device_id_type=MESH,
        )

    sent_stats = [
        along_z(1, d, stats.at[(req + d) % n_req], stat_in.at[d]) for d in range(1, n_req)
    ]
    sent_parts = [
        [
            along_z(0, d, parts.at[(req + d) % n_req, half], part_in.at[d, half], i)
            for d in range(1, n_req)
        ]
        for i, half in enumerate(halves)
    ]
    for copy in sent_stats + sent_parts[0] + sent_parts[1]:
        copy.start()
    part_in[0] = parts[req]
    stat_in[0] = stats[req]
    for copy in sent_stats:
        copy.wait()

    flat = stat_in[...].reshape(n_req * 2 * group, tokens)
    flat = jnp.concatenate([flat, jnp.zeros((128 - flat.shape[0], tokens), f32)], axis=0)
    columns = flat.T
    factors = []
    for j in range(group):
        at = [d * 2 * group + j for d in range(n_req)]
        peak = [columns[:, i : i + 1] for i in at]
        total_at = [columns[:, i + group : i + group + 1] for i in at]
        top = functools.reduce(jnp.maximum, peak)
        factor = [jnp.exp(p - top) for p in peak]
        inverse = 1.0 / sum(f * t for f, t in zip(factor, total_at))
        factors.append([f * inverse for f in factor])

    sent_heads = []
    for i, half in enumerate(halves):
        for copy in sent_parts[i]:
            copy.wait()
        for j in range(group):
            lanes = slice(j * value_width, (j + 1) * value_width)
            head = sum(
                part_in[d, half, lanes].astype(f32) * factors[j][d][half] for d in range(n_req)
            )
            head_in[0, half, lanes] = head.astype(bf16)
        sent_heads.append(
            [
                along_z(2, d, head_in.at[0, half], head_in.at[d, half], i)
                for d in range(1, n_req)
            ]
        )
        for copy in sent_heads[i]:
            copy.start()
    loads[0].wait()

    def project(delta, half):
        src = (req + n_req - delta) % n_req
        return jnp.dot(
            head_in[delta, half], out_proj[pl.ds(pl.multiple_of(src * width, width), width), :],
            preferred_element_type=f32,
        )

    sent_resid = []
    for i, half in enumerate(halves):
        attention = project(0, half)
        for d in range(1, n_req):
            sent_heads[i][d - 1].wait()
            attention = attention + project(d, half)
        resid_in[req, half] = (hidden[half].astype(f32) + attention).astype(bf16)
        sent_resid.append(
            [
                along_z(3, d, resid_in.at[req, half], resid_in.at[req, half], i)
                for d in range(1, n_req)
            ]
        )
        for copy in sent_resid[i]:
            copy.start()
    for copy in sent_resid[0] + sent_resid[1]:
        copy.wait()

    square = 0.0
    for d in range(n_req):
        wide = resid_in[d].astype(f32)
        square = square + jnp.sum(wide * wide, axis=1, keepdims=True)
    inverse = lax.rsqrt(square / (n_req * width) + 1e-06)
    for d in range(n_req):
        lanes = slice(d * width, (d + 1) * width)
        rows[0, 0, :, lanes] = (
            resid_in[d].astype(f32) * inverse * gain[:, lanes]
        ).astype(bf16)
    logits = across(router[...], rows[0, 0])
    lifted = named[...] / (1.0 + jnp.exp(-logits))
    gates[0, 0] = lifted / jnp.sum(lifted, axis=0, keepdims=True)

    def spread(s):
        to = (req, partner(s))
        return [
            pltpu.make_async_remote_copy(
                src_ref=buf.at[0, 0], dst_ref=buf.at[s, 0],
                send_sem=row_send.at[s, i], recv_sem=row_recv.at[s, i],
                device_id=to, device_id_type=MESH,
            )
            for i, buf in enumerate((rows, gates))
        ]

    def forward(s):
        return [
            pltpu.make_async_remote_copy(
                src_ref=buf.at[s, 0], dst_ref=buf.at[s, 1],
                send_sem=fwd_send.at[s, i], recv_sem=fwd_recv.at[s, i],
                device_id=(req, mate), device_id_type=MESH,
            )
            for i, buf in enumerate((rows, gates))
        ]

    def to_mate(s):
        return pltpu.make_async_remote_copy(
            src_ref=mate_out.at[s], dst_ref=mate_in.at[s],
            send_sem=mate_send.at[s], recv_sem=mate_recv.at[s],
            device_id=(req, mate), device_id_type=MESH,
        )

    def send_back(s):
        return pltpu.make_async_remote_copy(
            src_ref=back_out.at[s], dst_ref=back_in.at[s],
            send_sem=back_send.at[s], recv_sem=back_recv.at[s],
            device_id=(req, partner(s)), device_id_type=MESH,
        )

    last_after_first = chips > 2
    for s in range(1, chips - 1 if last_after_first else chips):
        for copy in spread(s):
            copy.start()
    for copy in forward(0):
        copy.start()

    def silu_times(value, lift):
        return value / (1.0 + jnp.exp(-value)) * lift

    loads[1].wait()
    loads[2].wait()
    shared_hidden = silu_times(
        across(rows[0, 0], shared_up[0]),
        across(rows[0, 0], shared_up[1]),
    ).astype(bf16)
    total[...] = jnp.dot(shared_hidden, shared_down[...], preferred_element_type=f32)
    loads[3].wait()
    loads[4].wait()

    def step(s, carry):
        @pl.when(s > 0)
        def _():
            for copy in spread(s):
                copy.wait_recv()
            for copy in forward(s):
                copy.start()

        if last_after_first:
            @pl.when(s == 1)
            def _():
                for copy in spread(chips - 1):
                    copy.start()

        for copy in forward(s):
            copy.wait_recv()
        both = rows[s].reshape(2 * tokens, n_req * width)
        own_gate = []
        for k in range(2):
            flat = gates[s, k]
            flat = jnp.concatenate([flat, jnp.zeros((128 - expert_total, tokens), f32)], axis=0)
            own_gate.append(flat.T)
        own_gate = jnp.concatenate(own_gate, axis=0)
        lane = lax.broadcasted_iota(jnp.int32, own_gate.shape, 1)
        weighted = []
        for e in range(local_experts):
            column = jnp.sum(
                jnp.where(lane == ep * local_experts + e, own_gate, 0.0), axis=1, keepdims=True
            )
            hidden_rows = silu_times(
                across(both, gate_up[e, 0]),
                across(both, gate_up[e, 1]),
            )
            weighted.append((hidden_rows * column).astype(bf16))

        def result(k):
            return sum(
                jnp.dot(
                    weighted[e][k * tokens : (k + 1) * tokens], down[e],
                    preferred_element_type=f32,
                )
                for e in range(local_experts)
            )

        mate_out[s] = result(1).astype(bf16)
        to_mate(s).start()
        own = result(0)
        to_mate(s).wait_recv()
        own = own + mate_in[s].astype(f32)

        @pl.when(s == 0)
        def _():
            total[...] += own

        @pl.when(s > 0)
        def _():
            back_out[s] = own.astype(bf16)
            send_back(s).start()

        return carry

    lax.fori_loop(0, chips, step, 0)
    summed = total[...]
    for s in range(1, chips):
        send_back(s).wait_recv()
        summed = summed + back_in[s].astype(f32)
    total[...] = summed
    for d in range(n_req):
        final_out[d] = summed[:, d * width : (d + 1) * width].astype(bf16)
    sent = []
    for delta in range(1, n_req):
        to = (req + delta) % n_req
        sent.append(along_z(4, delta, final_out.at[to], final_in.at[delta]))
    for copy in sent:
        copy.start()
    for s in range(chips):
        for copy in forward(s):
            copy.wait_send()
        to_mate(s).wait_send()
        if s:
            for copy in spread(s):
                copy.wait_send()
            send_back(s).wait_send()
    answer = resid_in[req].astype(f32) + final_out[req].astype(f32)
    for d in range(1, n_req):
        sent[d - 1].wait()
        answer = answer + final_in[d].astype(f32)
    out[...] = answer.astype(bf16)


def exchange(
    parts, stats, hidden, out_proj, gain, router, named, gate_up, down, shared_up, shared_down,
    n_req, n_ep,
):
    tokens, width = hidden.shape
    model = n_req * width
    chips = n_ep // 2
    bf16, f32 = jnp.bfloat16, jnp.float32
    in_vmem = pl.BlockSpec(memory_space=pltpu.VMEM)
    in_any = pl.BlockSpec(memory_space=pl.ANY)
    dma = pltpu.SemaphoreType.DMA
    weights = [out_proj, gate_up, down, shared_up, shared_down]
    return pl.pallas_call(
        functools.partial(exchange_kernel, n_req, n_ep),
        out_shape=jax.ShapeDtypeStruct((tokens, width), bf16),
        in_specs=[in_vmem] * 3 + [in_any] + [in_vmem] * 3 + [in_any] * 4,
        out_specs=in_vmem,
        scratch_shapes=[
            *[pltpu.VMEM(w.shape, w.dtype) for w in weights],
            dma((5,)),
            pltpu.VMEM(parts.shape, bf16),
            pltpu.VMEM(stats.shape, f32),
            pltpu.VMEM((n_req, tokens, width), bf16),
            pltpu.VMEM((n_req, tokens, width), bf16),
            pltpu.VMEM((n_req, tokens, width), bf16),
            pltpu.VMEM((n_req, tokens, width), bf16),
            dma((5, 2, n_req)),
            dma((5, 2, n_req)),
            pltpu.VMEM((chips, 2, tokens, model), bf16),
            pltpu.VMEM((chips, 2, named.shape[0], tokens), f32),
            pltpu.VMEM((chips, tokens, model), bf16),
            pltpu.VMEM((chips, tokens, model), bf16),
            pltpu.VMEM((chips, tokens, model), bf16),
            pltpu.VMEM((chips, tokens, model), bf16),
            pltpu.VMEM((tokens, model), f32),
            dma((chips, 2)),
            dma((chips, 2)),
            dma((chips, 2)),
            dma((chips, 2)),
            dma((chips,)),
            dma((chips,)),
            dma((chips,)),
            dma((chips,)),
        ],
        compiler_params=pltpu.CompilerParams(
            collective_id=0, has_side_effects=True, vmem_limit_bytes=56 * 1024 * 1024
        ),
    )(parts, stats, hidden, out_proj, gain, router, named, gate_up, down, shared_up, shared_down)


def ancestors(parents):
    draft_count = parents.shape[-1]
    draft_index = jnp.arange(draft_count, dtype=jnp.int32)
    ancestry = (parents[:, :, None] == draft_index[None, None, :]).astype(jnp.float32)
    ancestry = ancestry + jnp.eye(draft_count, dtype=jnp.float32)[None]
    for doubling in range(max(1, (draft_count - 1).bit_length())):
        ancestry = jnp.minimum(
            jnp.einsum("rij,rjk->rik", ancestry, ancestry, precision=lax.Precision.HIGHEST), 1.0
        )
    return ancestry


def per_device(
    queries,
    draft_latent,
    hidden_in,
    cache_pool,
    page_table,
    cache_len,
    parents,
    accept_leaf,
    absorb_key,
    absorb_value,
    out_proj,
    norm_gain,
    router,
    expert_ids,
    expert_gate_up,
    expert_down,
    shared_gate_up,
    shared_down,
):
    req_count = lax.axis_size("req")
    req_index = lax.axis_index("req")
    ep_count = lax.axis_size("ep")
    request_count, draft_count = parents.shape
    token_count = request_count * draft_count
    head_count = queries.shape[1]
    nope_width = absorb_key.shape[1]
    latent_width = absorb_key.shape[2]
    page_size = cache_pool.shape[1]
    page_count = page_table.shape[1]
    score_scale = 1.0 / math.sqrt(queries.shape[2])
    ancestry = ancestors(parents)
    depths = jnp.sum(ancestry, axis=2) - 1.0
    local_pages = page_count // req_count
    page_cols = req_index + req_count * jnp.arange(local_pages, dtype=jnp.int32)
    own_column = jnp.arange(req_count, dtype=jnp.int32) == req_index
    slot_rows = jnp.sum(
        jnp.where(own_column, page_table.reshape(request_count, local_pages, req_count), 0), axis=2
    )
    starts = cache_len // page_size
    page_now = starts + jnp.mod(req_index - starts, req_count)
    all_pages = jnp.arange(page_count, dtype=jnp.int32)
    slot_now = jnp.sum(
        jnp.where(all_pages[None, :] == page_now[:, None], page_table, 0), axis=1, keepdims=True
    )
    slots = jnp.concatenate([slot_rows, slot_now], axis=1)
    positions = (
        page_cols[:, None] * page_size + jnp.arange(page_size, dtype=jnp.int32)[None, :]
    ).reshape(-1)
    cache_bias = jnp.where(positions[None, :] < cache_len[:, None], 0.0, NEGATIVE)[:, None, :]
    draft_share = draft_count // req_count
    draft_index = jnp.arange(draft_count, dtype=jnp.int32)
    own_draft = draft_index // draft_share == req_index
    tree_bias = jnp.where((ancestry > 0.5) & own_draft[None, None, :], 0.0, NEGATIVE)
    same_request = jnp.eye(request_count, dtype=jnp.float32)
    tree_bias = jnp.where(
        same_request[:, None, :, None] > 0.5, tree_bias[:, :, None, :], NEGATIVE
    ).reshape(request_count, draft_count, token_count)
    offsets = (
        page_now[:, None] * page_size
        + jnp.arange(page_size, dtype=jnp.int32)[None, :]
        - cache_len[:, None]
    ).astype(jnp.float32)
    is_leaf = (draft_index[None, :] == accept_leaf[:, None]).astype(jnp.float32)
    accepted = jnp.sum(ancestry * is_leaf[:, :, None], axis=1)
    select = accepted[:, :, None] * (depths[:, :, None] == offsets[:, None, :]).astype(jnp.float32)
    touched = jnp.sum(select, axis=1, keepdims=True)
    select = (same_request[:, :, None, None] * select[:, None]).astype(jnp.bfloat16)
    select = select.reshape(request_count, token_count, page_size)
    absorbed = jnp.einsum(
        "thd,hdl->htl", queries[:, :, :nope_width], absorb_key, preferred_element_type=jnp.float32
    ).astype(jnp.bfloat16)
    rotary = jnp.transpose(queries[:, :, nope_width:], (1, 0, 2))
    projected, peaks, sums, fresh = attend(
        slots, absorbed, rotary, jnp.swapaxes(cache_pool, 1, 2), draft_latent.T, cache_bias,
        tree_bias, absorb_value, select, touched, score_scale, req_count,
    )
    local_experts = expert_gate_up.shape[0]
    expert_total = local_experts * ep_count
    named = jnp.any(
        expert_ids[:, :, None] == jnp.arange(expert_total, dtype=jnp.int32)[None, None, :], axis=1
    ).astype(jnp.float32)
    if ep_count <= 8:
        group = head_count // req_count
        by_head = jnp.stack([peaks[:, :head_count].T, sums[:, :head_count].T])
        by_head = by_head.reshape(2, req_count, group, token_count)
        by_head = jnp.transpose(by_head, (1, 0, 2, 3)).reshape(req_count, 2 * group, token_count)
        layer_out = exchange(
            projected, by_head, hidden_in, out_proj, norm_gain.reshape(1, -1), router.T, named.T,
            jnp.swapaxes(expert_gate_up, 2, 3), expert_down, jnp.swapaxes(shared_gate_up, 1, 2),
            shared_down, req_count, ep_count,
        )
    else:
        stats = lax.all_gather(jnp.stack([peaks, sums]), "req")
        parts = lax.all_gather(projected, "req").astype(jnp.float32)
        factors = jnp.exp(stats[:, 0] - jnp.max(stats[:, 0], axis=0)[None])
        factors = factors / jnp.sum(factors * stats[:, 1], axis=0)[None]
        factors = jnp.transpose(factors[..., :head_count], (0, 2, 1))
        parts = parts.reshape(req_count, req_count, token_count, head_count // req_count, -1)
        parts = jnp.transpose(parts, (0, 1, 3, 2, 4)).reshape(req_count, head_count, token_count, -1)
        head_out = jnp.transpose(jnp.sum(parts * factors[..., None], axis=0), (1, 0, 2))
        head_rows = head_out.astype(jnp.bfloat16).reshape(token_count, -1)
        attention = jnp.dot(head_rows, out_proj, preferred_element_type=jnp.float32)
        resid_cols = (hidden_in.astype(jnp.float32) + attention).astype(jnp.bfloat16)
        resid = lax.all_gather(resid_cols, "req", axis=1, tiled=True)
        resid_wide = resid.astype(jnp.float32)
        normed = resid_wide * lax.rsqrt(
            jnp.mean(resid_wide * resid_wide, axis=1, keepdims=True) + 1e-06
        )
        normed = (normed * norm_gain[None, :]).astype(jnp.bfloat16)
        everyone = lax.all_gather(normed, "ep", axis=0, tiled=True)
        logits = jnp.dot(normed, router, preferred_element_type=jnp.float32)
        lifted = jax.nn.sigmoid(logits) * named
        gates = lifted / jnp.sum(lifted, axis=1, keepdims=True)
        gates_all = lax.all_gather(gates, "ep", axis=0, tiled=True)
        own_gates = lax.dynamic_slice_in_dim(
            gates_all, lax.axis_index("ep") * local_experts, local_experts, axis=1
        )
        shared_gate = jnp.dot(normed, shared_gate_up[0], preferred_element_type=jnp.float32)
        shared_lift = jnp.dot(normed, shared_gate_up[1], preferred_element_type=jnp.float32)
        shared_hidden = (jax.nn.silu(shared_gate) * shared_lift).astype(jnp.bfloat16)
        shared_part = jnp.dot(shared_hidden, shared_down, preferred_element_type=jnp.float32)
        term = 0.0
        for e in range(local_experts):
            gate_value = jnp.dot(
                everyone, expert_gate_up[e, 0], preferred_element_type=jnp.float32
            )
            lift_value = jnp.dot(
                everyone, expert_gate_up[e, 1], preferred_element_type=jnp.float32
            )
            hidden_rows = (jax.nn.silu(gate_value) * lift_value).astype(jnp.bfloat16)
            result = jnp.dot(hidden_rows, expert_down[e], preferred_element_type=jnp.float32)
            term = term + own_gates[:, e : e + 1] * result
        routed = lax.psum_scatter(
            term.astype(jnp.bfloat16), "ep", scatter_dimension=0, tiled=True
        ).astype(jnp.float32)
        summed = lax.psum_scatter(
            (shared_part + routed).astype(jnp.bfloat16), "req", scatter_dimension=1, tiled=True
        ).astype(jnp.float32)
        layer_out = (resid_cols.astype(jnp.float32) + summed).astype(jnp.bfloat16)
    return (layer_out, jnp.swapaxes(fresh, 1, 2)[:, None])


def solution(mesh):
    in_specs = (
        P("ep", None, None),
        P("ep", None),
        P("ep", "req"),
        P(("req", "ep"), None, None),
        P("ep", None),
        P("ep"),
        P("ep", None),
        P("ep"),
        P(),
        P(),
        P(None, "req"),
        P(),
        P(),
        P("ep", None),
        P("ep", None, None, "req"),
        P("ep", "req", None),
        P(None, None, "req"),
        P("req", None),
    )
    out_specs = (P("ep", "req"), P("ep", "req", None, None))
    return jax.shard_map(
        per_device, mesh=mesh, in_specs=in_specs, out_specs=out_specs, check_vma=False
    )
```

```python
import functools
import math

import jax
import jax.numpy as jnp
from jax import lax
from jax.experimental import pallas as pl
from jax.experimental.pallas import tpu as pltpu
from jax.sharding import PartitionSpec as P

NEGATIVE = -1e30
FLOOR = -1e29
MESH = pl.DeviceIdType.MESH


def attend_kernel(scale, page_count, slots, absorbed, rotary, *rest):
    pages = rest[:page_count]
    old_page, drafts, cache_bias, tree_bias, value, select, touched = rest[page_count:-6]
    projected, peaks, sums, fresh, keys, bias = rest[-6:]
    page_size = pages[0].shape[2]
    cached = page_count * page_size
    draft_count = tree_bias.shape[1]
    latent_width = absorbed.shape[2]
    head_count = absorbed.shape[0]
    group = head_count // projected.shape[0]
    value_width = value.shape[2]
    for p in range(page_count):
        keys[:, p * page_size : (p + 1) * page_size] = pages[p][0]
    keys[:, cached:] = drafts[...]
    written = jnp.dot(drafts[...], select[0], preferred_element_type=jnp.float32)
    fresh[0] = jnp.where(
        touched[0] > 0.5, written, old_page[0].astype(jnp.float32)
    ).astype(jnp.bfloat16)
    bias[:, :cached] = jnp.broadcast_to(cache_bias[0], (draft_count, cached))
    bias[:, cached:] = tree_bias[0]
    contract_last = (((1,), (1,)), ((), ()))
    peaks[...] = jnp.zeros_like(peaks)
    sums[...] = jnp.ones_like(sums)

    for chunk in range(head_count // group):
        rows = slice(chunk * group, (chunk + 1) * group)
        nope = absorbed[rows].reshape(group * draft_count, latent_width)
        rope = rotary[rows].reshape(group * draft_count, rotary.shape[2])
        scores = jnp.dot(
            nope, keys[:latent_width, :], preferred_element_type=jnp.float32
        ) + jnp.dot(rope, keys[latent_width:, :], preferred_element_type=jnp.float32)
        scores = scores.reshape(group, draft_count, -1) * scale + bias[...][None]
        scores = scores.reshape(group * draft_count, -1)
        peak = jnp.maximum(jnp.max(scores, axis=1, keepdims=True), FLOOR)
        weights = jnp.exp(scores - peak)
        total = jnp.sum(weights, axis=1, keepdims=True)
        mixed = lax.dot_general(
            weights.astype(jnp.bfloat16), keys[:latent_width, :], contract_last,
            preferred_element_type=jnp.float32,
        ).astype(jnp.bfloat16)
        for j in range(group):
            h = chunk * group + j
            own = slice(j * draft_count, (j + 1) * draft_count)
            projected[chunk, :, j * value_width : (j + 1) * value_width] = jnp.dot(
                mixed[own], value[h], preferred_element_type=jnp.float32
            ).astype(jnp.bfloat16)
            peaks[:, h : h + 1] = peak[own]
            sums[:, h : h + 1] = total[own]


def attend(
    slots, absorbed, rotary, pool, drafts, cache_bias, tree_bias, value, select, touched, scale,
    chunks,
):
    requests, page_count = slots.shape[0], slots.shape[1] - 1
    heads, tokens, latent_width = absorbed.shape
    key_width, page_size = pool.shape[1:]
    draft_count = tree_bias.shape[1]
    width = heads // chunks * value.shape[2]
    cached = page_count * page_size

    def page_spec(p):
        return pl.BlockSpec((1, key_width, page_size), lambda r, table: (table[r, p], 0, 0))

    def by_request(shape):
        return pl.BlockSpec((1,) + shape, lambda r, table: (r, 0, 0))

    return pl.pallas_call(
        functools.partial(attend_kernel, scale, page_count),
        grid_spec=pltpu.PrefetchScalarGridSpec(
            num_scalar_prefetch=1,
            grid=(requests,),
            in_specs=[
                pl.BlockSpec((heads, draft_count, latent_width), lambda r, table: (0, r, 0)),
                pl.BlockSpec((heads, draft_count, rotary.shape[2]), lambda r, table: (0, r, 0)),
                *[page_spec(p) for p in range(page_count + 1)],
                pl.BlockSpec(drafts.shape, lambda r, table: (0, 0)),
                by_request((1, cached)),
                by_request((draft_count, tokens)),
                pl.BlockSpec(value.shape, lambda r, table: (0, 0, 0)),
                by_request((tokens, page_size)),
                by_request((1, page_size)),
            ],
            out_specs=[
                pl.BlockSpec((chunks, draft_count, width), lambda r, table: (0, r, 0)),
                pl.BlockSpec((draft_count, 128), lambda r, table: (r, 0)),
                pl.BlockSpec((draft_count, 128), lambda r, table: (r, 0)),
                by_request((key_width, page_size)),
            ],
            scratch_shapes=[
                pltpu.VMEM((key_width, cached + tokens), jnp.bfloat16),
                pltpu.VMEM((draft_count, cached + tokens), jnp.float32),
            ],
        ),
        out_shape=[
            jax.ShapeDtypeStruct((chunks, tokens, width), jnp.bfloat16),
            jax.ShapeDtypeStruct((tokens, 128), jnp.float32),
            jax.ShapeDtypeStruct((tokens, 128), jnp.float32),
            jax.ShapeDtypeStruct((requests, key_width, page_size), jnp.bfloat16),
        ],
        compiler_params=pltpu.CompilerParams(vmem_limit_bytes=58 * 1024 * 1024),
    )(
        slots, absorbed, rotary, *[pool] * (page_count + 1), drafts, cache_bias, tree_bias, value,
        select, touched,
    )


def exchange_kernel(
    n_req, n_ep, parts, stats, hidden, out_proj_hbm, gain, router, named, gate_up_hbm, down_hbm,
    shared_up_hbm, shared_down_hbm, out,
    out_proj, gate_up, down, shared_up, shared_down, weight_sem,
    part_in, stat_in, head_in, resid_in, final_out, final_in, z_send, z_recv,
    rows, gates, mate_out, mate_in, back_out, back_in, total,
    row_send, row_recv, fwd_send, fwd_recv, mate_send, mate_recv, back_send, back_recv,
):
    f32, bf16 = jnp.float32, jnp.bfloat16
    req = lax.axis_index("req")
    ep = lax.axis_index("ep")
    chips = n_ep // 2
    core = ep % 2
    chip = ep // 2
    mate = chip * 2 + 1 - core
    tokens, width = hidden.shape
    group = stats.shape[1] // 2
    value_width = width // group
    expert_total = named.shape[0]
    local_experts = gate_up.shape[0]

    def across(left, right):
        return lax.dot_general(
            left, right, (((1,), (1,)), ((), ())), preferred_element_type=f32
        )

    def partner(s):
        there, bit = 0, 1
        while bit < chips:
            there = there + bit * (((chip // bit) % 2 + (s // bit) % 2) % 2)
            bit *= 2
        return there * 2 + core

    loads = [
        pltpu.make_async_copy(src, dst, weight_sem.at[i])
        for i, (src, dst) in enumerate(
            [
                (out_proj_hbm, out_proj),
                (shared_up_hbm, shared_up),
                (shared_down_hbm, shared_down),
                (gate_up_hbm, gate_up),
                (down_hbm, down),
            ]
        )
    ]
    for load in loads:
        load.start()

    barrier = pltpu.get_barrier_semaphore()
    for delta in range(1, n_req):
        pl.semaphore_signal(
            barrier, inc=1, device_id=((req + delta) % n_req, ep), device_id_type=MESH
        )
    for s in range(1, chips):
        pl.semaphore_signal(barrier, inc=1, device_id=(req, partner(s)), device_id_type=MESH)
    pl.semaphore_signal(barrier, inc=1, device_id=(req, mate), device_id_type=MESH)
    pl.semaphore_wait(barrier, n_req - 1 + chips)

    halves = [slice(0, tokens // 2), slice(tokens // 2, tokens)]

    def along_z(stage, delta, src, dst, half=0):
        return pltpu.make_async_remote_copy(
            src_ref=src, dst_ref=dst,
            send_sem=z_send.at[stage, half, delta], recv_sem=z_recv.at[stage, half, delta],
            device_id=((req + delta) % n_req, ep), device_id_type=MESH,
        )

    sent_stats = [
        along_z(1, d, stats.at[(req + d) % n_req], stat_in.at[d]) for d in range(1, n_req)
    ]
    sent_parts = [
        [
            along_z(0, d, parts.at[(req + d) % n_req, half], part_in.at[d, half], i)
            for d in range(1, n_req)
        ]
        for i, half in enumerate(halves)
    ]
    for copy in sent_stats + sent_parts[0] + sent_parts[1]:
        copy.start()
    part_in[0] = parts[req]
    stat_in[0] = stats[req]
    for copy in sent_stats:
        copy.wait()

    flat = stat_in[...].reshape(n_req * 2 * group, tokens)
    flat = jnp.concatenate([flat, jnp.zeros((128 - flat.shape[0], tokens), f32)], axis=0)
    columns = flat.T
    factors = []
    for j in range(group):
        at = [d * 2 * group + j for d in range(n_req)]
        peak = [columns[:, i : i + 1] for i in at]
        total_at = [columns[:, i + group : i + group + 1] for i in at]
        top = functools.reduce(jnp.maximum, peak)
        factor = [jnp.exp(p - top) for p in peak]
        inverse = 1.0 / sum(f * t for f, t in zip(factor, total_at))
        factors.append([f * inverse for f in factor])

    sent_heads = []
    for i, half in enumerate(halves):
        for copy in sent_parts[i]:
            copy.wait()
        for j in range(group):
            lanes = slice(j * value_width, (j + 1) * value_width)
            head = sum(
                part_in[d, half, lanes].astype(f32) * factors[j][d][half] for d in range(n_req)
            )
            head_in[0, half, lanes] = head.astype(bf16)
        sent_heads.append(
            [
                along_z(2, d, head_in.at[0, half], head_in.at[d, half], i)
                for d in range(1, n_req)
            ]
        )
        for copy in sent_heads[i]:
            copy.start()
    loads[0].wait()

    def project(delta, half):
        src = (req + n_req - delta) % n_req
        return jnp.dot(
            head_in[delta, half], out_proj[pl.ds(pl.multiple_of(src * width, width), width), :],
            preferred_element_type=f32,
        )

    sent_resid = []
    for i, half in enumerate(halves):
        attention = project(0, half)
        for d in range(1, n_req):
            sent_heads[i][d - 1].wait()
            attention = attention + project(d, half)
        resid_in[req, half] = (hidden[half].astype(f32) + attention).astype(bf16)
        sent_resid.append(
            [
                along_z(3, d, resid_in.at[req, half], resid_in.at[req, half], i)
                for d in range(1, n_req)
            ]
        )
        for copy in sent_resid[i]:
            copy.start()
    for copy in sent_resid[0] + sent_resid[1]:
        copy.wait()

    square = 0.0
    for d in range(n_req):
        wide = resid_in[d].astype(f32)
        square = square + jnp.sum(wide * wide, axis=1, keepdims=True)
    inverse = lax.rsqrt(square / (n_req * width) + 1e-06)
    for d in range(n_req):
        lanes = slice(d * width, (d + 1) * width)
        rows[0, 0, :, lanes] = (
            resid_in[d].astype(f32) * inverse * gain[:, lanes]
        ).astype(bf16)
    logits = across(router[...], rows[0, 0])
    lifted = named[...] / (1.0 + jnp.exp(-logits))
    gates[0, 0] = lifted / jnp.sum(lifted, axis=0, keepdims=True)

    def spread(s):
        to = (req, partner(s))
        return [
            pltpu.make_async_remote_copy(
                src_ref=buf.at[0, 0], dst_ref=buf.at[s, 0],
                send_sem=row_send.at[s, i], recv_sem=row_recv.at[s, i],
                device_id=to, device_id_type=MESH,
            )
            for i, buf in enumerate((rows, gates))
        ]

    def forward(s):
        return [
            pltpu.make_async_remote_copy(
                src_ref=buf.at[s, 0], dst_ref=buf.at[s, 1],
                send_sem=fwd_send.at[s, i], recv_sem=fwd_recv.at[s, i],
                device_id=(req, mate), device_id_type=MESH,
            )
            for i, buf in enumerate((rows, gates))
        ]

    def to_mate(s):
        return pltpu.make_async_remote_copy(
            src_ref=mate_out.at[s], dst_ref=mate_in.at[s],
            send_sem=mate_send.at[s], recv_sem=mate_recv.at[s],
            device_id=(req, mate), device_id_type=MESH,
        )

    def send_back(s):
        return pltpu.make_async_remote_copy(
            src_ref=back_out.at[s], dst_ref=back_in.at[s],
            send_sem=back_send.at[s], recv_sem=back_recv.at[s],
            device_id=(req, partner(s)), device_id_type=MESH,
        )

    last_after_first = chips > 2
    for s in range(1, chips - 1 if last_after_first else chips):
        for copy in spread(s):
            copy.start()
    for copy in forward(0):
        copy.start()

    def silu_times(value, lift):
        return value / (1.0 + jnp.exp(-value)) * lift

    loads[1].wait()
    loads[2].wait()
    shared_hidden = silu_times(
        across(rows[0, 0], shared_up[0]),
        across(rows[0, 0], shared_up[1]),
    ).astype(bf16)
    total[...] = jnp.dot(shared_hidden, shared_down[...], preferred_element_type=f32)
    loads[3].wait()
    loads[4].wait()

    def step(s, carry):
        if last_after_first:
            @pl.when(s == 1)
            def _():
                for copy in spread(1):
                    copy.wait_recv()
                for copy in forward(1):
                    copy.start()
                for copy in spread(chips - 1):
                    copy.start()
                for early in range(2, chips - 1):
                    for copy in spread(early):
                        copy.wait_recv()
                    for copy in forward(early):
                        copy.start()

        @pl.when(s == chips - 1 if last_after_first else s > 0)
        def _():
            for copy in spread(s):
                copy.wait_recv()
            for copy in forward(s):
                copy.start()

        for copy in forward(s):
            copy.wait_recv()
        both = rows[s].reshape(2 * tokens, n_req * width)
        own_gate = []
        for k in range(2):
            flat = gates[s, k]
            flat = jnp.concatenate([flat, jnp.zeros((128 - expert_total, tokens), f32)], axis=0)
            own_gate.append(flat.T)
        own_gate = jnp.concatenate(own_gate, axis=0)
        lane = lax.broadcasted_iota(jnp.int32, own_gate.shape, 1)
        weighted = []
        for e in range(local_experts):
            column = jnp.sum(
                jnp.where(lane == ep * local_experts + e, own_gate, 0.0), axis=1, keepdims=True
            )
            hidden_rows = silu_times(
                across(both, gate_up[e, 0]),
                across(both, gate_up[e, 1]),
            )
            weighted.append((hidden_rows * column).astype(bf16))

        def result(k):
            return sum(
                jnp.dot(
                    weighted[e][k * tokens : (k + 1) * tokens], down[e],
                    preferred_element_type=f32,
                )
                for e in range(local_experts)
            )

        mate_out[s] = result(1).astype(bf16)
        to_mate(s).start()
        own = result(0)
        to_mate(s).wait_recv()
        own = own + mate_in[s].astype(f32)

        @pl.when(s == 0)
        def _():
            total[...] += own

        @pl.when(s > 0)
        def _():
            back_out[s] = own.astype(bf16)
            send_back(s).start()

        return carry

    lax.fori_loop(0, chips, step, 0)
    summed = total[...]
    for s in range(1, chips):
        send_back(s).wait_recv()
        summed = summed + back_in[s].astype(f32)
    total[...] = summed
    for d in range(n_req):
        final_out[d] = summed[:, d * width : (d + 1) * width].astype(bf16)
    sent = []
    for delta in range(1, n_req):
        to = (req + delta) % n_req
        sent.append(along_z(4, delta, final_out.at[to], final_in.at[delta]))
    for copy in sent:
        copy.start()
    for s in range(chips):
        for copy in forward(s):
            copy.wait_send()
        to_mate(s).wait_send()
        if s:
            for copy in spread(s):
                copy.wait_send()
            send_back(s).wait_send()
    answer = resid_in[req].astype(f32) + final_out[req].astype(f32)
    for d in range(1, n_req):
        sent[d - 1].wait()
        answer = answer + final_in[d].astype(f32)
    out[...] = answer.astype(bf16)


def exchange(
    parts, stats, hidden, out_proj, gain, router, named, gate_up, down, shared_up, shared_down,
    n_req, n_ep,
):
    tokens, width = hidden.shape
    model = n_req * width
    chips = n_ep // 2
    bf16, f32 = jnp.bfloat16, jnp.float32
    in_vmem = pl.BlockSpec(memory_space=pltpu.VMEM)
    in_any = pl.BlockSpec(memory_space=pl.ANY)
    dma = pltpu.SemaphoreType.DMA
    weights = [out_proj, gate_up, down, shared_up, shared_down]
    return pl.pallas_call(
        functools.partial(exchange_kernel, n_req, n_ep),
        out_shape=jax.ShapeDtypeStruct((tokens, width), bf16),
        in_specs=[in_vmem] * 3 + [in_any] + [in_vmem] * 3 + [in_any] * 4,
        out_specs=in_vmem,
        scratch_shapes=[
            *[pltpu.VMEM(w.shape, w.dtype) for w in weights],
            dma((5,)),
            pltpu.VMEM(parts.shape, bf16),
            pltpu.VMEM(stats.shape, f32),
            pltpu.VMEM((n_req, tokens, width), bf16),
            pltpu.VMEM((n_req, tokens, width), bf16),
            pltpu.VMEM((n_req, tokens, width), bf16),
            pltpu.VMEM((n_req, tokens, width), bf16),
            dma((5, 2, n_req)),
            dma((5, 2, n_req)),
            pltpu.VMEM((chips, 2, tokens, model), bf16),
            pltpu.VMEM((chips, 2, named.shape[0], tokens), f32),
            pltpu.VMEM((chips, tokens, model), bf16),
            pltpu.VMEM((chips, tokens, model), bf16),
            pltpu.VMEM((chips, tokens, model), bf16),
            pltpu.VMEM((chips, tokens, model), bf16),
            pltpu.VMEM((tokens, model), f32),
            dma((chips, 2)),
            dma((chips, 2)),
            dma((chips, 2)),
            dma((chips, 2)),
            dma((chips,)),
            dma((chips,)),
            dma((chips,)),
            dma((chips,)),
        ],
        compiler_params=pltpu.CompilerParams(
            collective_id=0, has_side_effects=True, vmem_limit_bytes=56 * 1024 * 1024
        ),
    )(parts, stats, hidden, out_proj, gain, router, named, gate_up, down, shared_up, shared_down)


def ancestors(parents):
    draft_count = parents.shape[-1]
    draft_index = jnp.arange(draft_count, dtype=jnp.int32)
    ancestry = (parents[:, :, None] == draft_index[None, None, :]).astype(jnp.float32)
    ancestry = ancestry + jnp.eye(draft_count, dtype=jnp.float32)[None]
    for doubling in range(max(1, (draft_count - 1).bit_length())):
        ancestry = jnp.minimum(
            jnp.einsum("rij,rjk->rik", ancestry, ancestry, precision=lax.Precision.HIGHEST), 1.0
        )
    return ancestry


def per_device(
    queries,
    draft_latent,
    hidden_in,
    cache_pool,
    page_table,
    cache_len,
    parents,
    accept_leaf,
    absorb_key,
    absorb_value,
    out_proj,
    norm_gain,
    router,
    expert_ids,
    expert_gate_up,
    expert_down,
    shared_gate_up,
    shared_down,
):
    req_count = lax.axis_size("req")
    req_index = lax.axis_index("req")
    ep_count = lax.axis_size("ep")
    request_count, draft_count = parents.shape
    token_count = request_count * draft_count
    head_count = queries.shape[1]
    nope_width = absorb_key.shape[1]
    latent_width = absorb_key.shape[2]
    page_size = cache_pool.shape[1]
    page_count = page_table.shape[1]
    score_scale = 1.0 / math.sqrt(queries.shape[2])
    ancestry = ancestors(parents)
    depths = jnp.sum(ancestry, axis=2) - 1.0
    local_pages = page_count // req_count
    page_cols = req_index + req_count * jnp.arange(local_pages, dtype=jnp.int32)
    own_column = jnp.arange(req_count, dtype=jnp.int32) == req_index
    slot_rows = jnp.sum(
        jnp.where(own_column, page_table.reshape(request_count, local_pages, req_count), 0), axis=2
    )
    starts = cache_len // page_size
    page_now = starts + jnp.mod(req_index - starts, req_count)
    all_pages = jnp.arange(page_count, dtype=jnp.int32)
    slot_now = jnp.sum(
        jnp.where(all_pages[None, :] == page_now[:, None], page_table, 0), axis=1, keepdims=True
    )
    slots = jnp.concatenate([slot_rows, slot_now], axis=1)
    positions = (
        page_cols[:, None] * page_size + jnp.arange(page_size, dtype=jnp.int32)[None, :]
    ).reshape(-1)
    cache_bias = jnp.where(positions[None, :] < cache_len[:, None], 0.0, NEGATIVE)[:, None, :]
    draft_share = draft_count // req_count
    draft_index = jnp.arange(draft_count, dtype=jnp.int32)
    own_draft = draft_index // draft_share == req_index
    tree_bias = jnp.where((ancestry > 0.5) & own_draft[None, None, :], 0.0, NEGATIVE)
    same_request = jnp.eye(request_count, dtype=jnp.float32)
    tree_bias = jnp.where(
        same_request[:, None, :, None] > 0.5, tree_bias[:, :, None, :], NEGATIVE
    ).reshape(request_count, draft_count, token_count)
    offsets = (
        page_now[:, None] * page_size
        + jnp.arange(page_size, dtype=jnp.int32)[None, :]
        - cache_len[:, None]
    ).astype(jnp.float32)
    is_leaf = (draft_index[None, :] == accept_leaf[:, None]).astype(jnp.float32)
    accepted = jnp.sum(ancestry * is_leaf[:, :, None], axis=1)
    select = accepted[:, :, None] * (depths[:, :, None] == offsets[:, None, :]).astype(jnp.float32)
    touched = jnp.sum(select, axis=1, keepdims=True)
    select = (same_request[:, :, None, None] * select[:, None]).astype(jnp.bfloat16)
    select = select.reshape(request_count, token_count, page_size)
    absorbed = jnp.einsum(
        "thd,hdl->htl", queries[:, :, :nope_width], absorb_key, preferred_element_type=jnp.float32
    ).astype(jnp.bfloat16)
    rotary = jnp.transpose(queries[:, :, nope_width:], (1, 0, 2))
    projected, peaks, sums, fresh = attend(
        slots, absorbed, rotary, jnp.swapaxes(cache_pool, 1, 2), draft_latent.T, cache_bias,
        tree_bias, absorb_value, select, touched, score_scale, req_count,
    )
    local_experts = expert_gate_up.shape[0]
    expert_total = local_experts * ep_count
    named = jnp.any(
        expert_ids[:, :, None] == jnp.arange(expert_total, dtype=jnp.int32)[None, None, :], axis=1
    ).astype(jnp.float32)
    if ep_count <= 8:
        group = head_count // req_count
        by_head = jnp.stack([peaks[:, :head_count].T, sums[:, :head_count].T])
        by_head = by_head.reshape(2, req_count, group, token_count)
        by_head = jnp.transpose(by_head, (1, 0, 2, 3)).reshape(req_count, 2 * group, token_count)
        layer_out = exchange(
            projected, by_head, hidden_in, out_proj, norm_gain.reshape(1, -1), router.T, named.T,
            jnp.swapaxes(expert_gate_up, 2, 3), expert_down, jnp.swapaxes(shared_gate_up, 1, 2),
            shared_down, req_count, ep_count,
        )
    else:
        stats = lax.all_gather(jnp.stack([peaks, sums]), "req")
        parts = lax.all_gather(projected, "req").astype(jnp.float32)
        factors = jnp.exp(stats[:, 0] - jnp.max(stats[:, 0], axis=0)[None])
        factors = factors / jnp.sum(factors * stats[:, 1], axis=0)[None]
        factors = jnp.transpose(factors[..., :head_count], (0, 2, 1))
        parts = parts.reshape(req_count, req_count, token_count, head_count // req_count, -1)
        parts = jnp.transpose(parts, (0, 1, 3, 2, 4)).reshape(req_count, head_count, token_count, -1)
        head_out = jnp.transpose(jnp.sum(parts * factors[..., None], axis=0), (1, 0, 2))
        head_rows = head_out.astype(jnp.bfloat16).reshape(token_count, -1)
        attention = jnp.dot(head_rows, out_proj, preferred_element_type=jnp.float32)
        resid_cols = (hidden_in.astype(jnp.float32) + attention).astype(jnp.bfloat16)
        resid = lax.all_gather(resid_cols, "req", axis=1, tiled=True)
        resid_wide = resid.astype(jnp.float32)
        normed = resid_wide * lax.rsqrt(
            jnp.mean(resid_wide * resid_wide, axis=1, keepdims=True) + 1e-06
        )
        normed = (normed * norm_gain[None, :]).astype(jnp.bfloat16)
        everyone = lax.all_gather(normed, "ep", axis=0, tiled=True)
        logits = jnp.dot(normed, router, preferred_element_type=jnp.float32)
        lifted = jax.nn.sigmoid(logits) * named
        gates = lifted / jnp.sum(lifted, axis=1, keepdims=True)
        gates_all = lax.all_gather(gates, "ep", axis=0, tiled=True)
        own_gates = lax.dynamic_slice_in_dim(
            gates_all, lax.axis_index("ep") * local_experts, local_experts, axis=1
        )
        shared_gate = jnp.dot(normed, shared_gate_up[0], preferred_element_type=jnp.float32)
        shared_lift = jnp.dot(normed, shared_gate_up[1], preferred_element_type=jnp.float32)
        shared_hidden = (jax.nn.silu(shared_gate) * shared_lift).astype(jnp.bfloat16)
        shared_part = jnp.dot(shared_hidden, shared_down, preferred_element_type=jnp.float32)
        term = 0.0
        for e in range(local_experts):
            gate_value = jnp.dot(
                everyone, expert_gate_up[e, 0], preferred_element_type=jnp.float32
            )
            lift_value = jnp.dot(
                everyone, expert_gate_up[e, 1], preferred_element_type=jnp.float32
            )
            hidden_rows = (jax.nn.silu(gate_value) * lift_value).astype(jnp.bfloat16)
            result = jnp.dot(hidden_rows, expert_down[e], preferred_element_type=jnp.float32)
            term = term + own_gates[:, e : e + 1] * result
        routed = lax.psum_scatter(
            term.astype(jnp.bfloat16), "ep", scatter_dimension=0, tiled=True
        ).astype(jnp.float32)
        summed = lax.psum_scatter(
            (shared_part + routed).astype(jnp.bfloat16), "req", scatter_dimension=1, tiled=True
        ).astype(jnp.float32)
        layer_out = (resid_cols.astype(jnp.float32) + summed).astype(jnp.bfloat16)
    return (layer_out, jnp.swapaxes(fresh, 1, 2)[:, None])


def solution(mesh):
    in_specs = (
        P("ep", None, None),
        P("ep", None),
        P("ep", "req"),
        P(("req", "ep"), None, None),
        P("ep", None),
        P("ep"),
        P("ep", None),
        P("ep"),
        P(),
        P(),
        P(None, "req"),
        P(),
        P(),
        P("ep", None),
        P("ep", None, None, "req"),
        P("ep", "req", None),
        P(None, None, "req"),
        P("req", None),
    )
    out_specs = (P("ep", "req"), P("ep", "req", None, None))
    return jax.shard_map(
        per_device, mesh=mesh, in_specs=in_specs, out_specs=out_specs, check_vma=False
    )
```
